32 devices in a mesh: dp: 8 (over y, x, core), blk: 4 (over z).
Axes of the slice: x: 2, y: 2, z: 4, core: 2. Of those that a mesh axis runs over, the one named last changes fastest.
Arguments:
- speech: bfloat16 [16, 864, 768], P('dp', 'blk'), may hold values from -6 to 6
- lengths: int32 [16], P('dp'), may hold values from 144 to 864, as said below
- grad_output: bfloat16 [16, 864, 768], P('dp', 'blk'), may hold values from -6 to 6
- w_qkv: bfloat16 [768, 2304], replicated, may hold values from -0.3125 to 0.3125
- bias_query: float32 [768], replicated, may hold values from -2 to 2
- bias_value: float32 [768], replicated, may hold values from -2 to 2
- w_out: bfloat16 [768, 768], replicated, may hold values from -0.875 to 0.875
- bias_out: float32 [768], replicated, may hold values from -2 to 2
- gain_first: float32 [768], replicated, may hold values from 0.1 to 1.9
- shift_first: float32 [768], replicated, may hold values from -2 to 2
- w_up: bfloat16 [768, 3072], replicated, may hold values from -0.21875 to 0.21875
- bias_up: float32 [3072], replicated, may hold values from -2 to 2
- w_down: bfloat16 [3072, 768], replicated, may hold values from -0.109375 to 0.109375
- bias_down: float32 [768], replicated, may hold values from -2 to 2
- gain_second: float32 [768], replicated, may hold values from 0.1 to 1.9
- shift_second: float32 [768], replicated, may hold values from -2 to 2
Outputs:
- output: bfloat16 [16, 864, 768], P('dp', 'blk')
- grad_speech: float32 [16, 864, 768], P('dp', 'blk')
- grad_w_qkv: float32 [768, 2304], P('dp', 'blk')
- grad_bias_query: float32 [768], replicated
- grad_bias_value: float32 [768], replicated
- grad_w_out: float32 [768, 768], P('dp', 'blk')
- grad_bias_out: float32 [768], replicated
- grad_gain_first: float32 [768], replicated
- grad_shift_first: float32 [768], replicated
- grad_w_up: float32 [768, 3072], P('dp', 'blk')
- grad_bias_up: float32 [3072], replicated
- grad_w_down: float32 [3072, 768], P('dp', 'blk')
- grad_bias_down: float32 [768], replicated
- grad_gain_second: float32 [768], replicated
- grad_shift_second: float32 [768], replicated
The draws below stay inside these ranges and needn't reach their ends.
Inputs may be any that keep to these rules, and one draw needn't show every extreme that they name: `lengths`: in each group of 2 utterances held by one index of dp, one has all 864 frames.
All inputs are finite; a program needn't handle non-finite values.
Results may differ from the reference program's by a relative error of at most 0.019.
Values may be sent and summed in bfloat16 or wider, within the bound.
A program may use at most 192 MiB of HBM per device.

```python
import jax
import jax.numpy as jnp
from jax import lax

D = 768
H = 12
DH = 64
FF = 3072
FRAMES = 864
UTT_DEV = 2
UTTS = 16


def draw_lengths(key, part):
    key = jax.random.fold_in(key, 11)
    first_key, second_key = jax.random.split(key)
    drawn_len = jax.random.randint(first_key, (UTTS,), FRAMES // 6, FRAMES + 1)
    chosen = jax.random.randint(second_key, (UTTS // UTT_DEV,), 0, UTT_DEV)
    slot_index = jnp.arange(UTTS) % UTT_DEV
    picked = jnp.repeat(chosen, UTT_DEV, total_repeat_length=UTTS)
    return jnp.where(slot_index == picked, FRAMES, drawn_len).astype(jnp.int32)


def draw_grad_output(key, part):
    key = jax.random.fold_in(key, 23)
    first_key = jax.random.fold_in(key, 0)
    position = (jnp.arange(UTTS, dtype=jnp.float32)[:, None] * FRAMES + jnp.arange(FRAMES, dtype=jnp.float32)[None, :]) / (UTTS * FRAMES)
    row_scale = (0.5 + position)[:, :, None]
    values = jax.random.truncated_normal(first_key, -4.0, 4.0, (UTTS, FRAMES, D), jnp.float32) * row_scale
    return values.astype(jnp.bfloat16)


def block_scale(stream_key, shape, cuts, smallest, largest):
    factor_of, own = 1.0, jax.random.fold_in(stream_key, 6)
    for axis_at, parts in cuts:
        steps = jnp.exp(jax.random.uniform(jax.random.fold_in(own, axis_at), (parts,), jnp.float32, smallest / len(cuts), largest / len(cuts)))
        factor_of = factor_of * jnp.repeat(steps, shape[axis_at] // parts).reshape([-1 if axis == axis_at else 1 for axis in range(len(shape))])
    return factor_of


def gaussian(own_key, shape, deviation, reach, cuts=(), held_as=jnp.bfloat16):
    entries = jax.random.normal(own_key, shape, jnp.float32) * deviation
    if len(cuts) > 0:
        entries = block_scale(own_key, shape, cuts, -0.22, 0.18) * entries
    return jnp.clip(entries, min=-reach, max=reach).astype(held_as)


def setup_inputs(seed: int = 0) -> dict:
    key_of = jax.random.split(jax.random.key(seed), 17)
    speech = gaussian(key_of[0], (UTTS, FRAMES, D), 1.0, 6.0, ((0, 8), (1, 4)))
    lengths = draw_lengths(jax.random.fold_in(key_of[16], 71), 0)
    grad_output = draw_grad_output(jax.random.fold_in(key_of[16], 71), 0)
    w_qkv = gaussian(key_of[3], (D, 3 * D), (D // 2) ** -0.5, 0.3125)
    bias_query = gaussian(key_of[4], (D,), 0.3, 2.0, (), jnp.float32)
    bias_value = gaussian(key_of[5], (D,), 0.3, 2.0, (), jnp.float32)
    w_out = gaussian(key_of[6], (D, D), (D // 16) ** -0.5, 0.875)
    bias_out = gaussian(key_of[7], (D,), 0.3, 2.0, (), jnp.float32)
    gain_first = jnp.clip(1.0 + 0.18 * jax.random.normal(key_of[8], (D,), jnp.float32), 0.1, 1.9)
    shift_first = gaussian(key_of[9], (D,), 0.3, 2.0, (), jnp.float32)
    w_up = gaussian(key_of[10], (D, FF), D ** -0.5, 0.21875)
    bias_up = gaussian(key_of[11], (FF,), 0.3, 2.0, (), jnp.float32)
    w_down = gaussian(key_of[12], (FF, D), FF ** -0.5, 0.109375)
    bias_down = gaussian(key_of[13], (D,), 0.3, 2.0, (), jnp.float32)
    gain_second = jnp.clip(1.0 + 0.18 * jax.random.normal(key_of[14], (D,), jnp.float32), 0.1, 1.9)
    shift_second = gaussian(key_of[15], (D,), 0.3, 2.0, (), jnp.float32)
    return {"speech": speech, "lengths": lengths, "grad_output": grad_output, "w_qkv": w_qkv, "bias_query": bias_query, "bias_value": bias_value, "w_out": w_out, "bias_out": bias_out, "gain_first": gain_first, "shift_first": shift_first, "w_up": w_up, "bias_up": bias_up, "w_down": w_down, "bias_down": bias_down, "gain_second": gain_second, "shift_second": shift_second}


@jax.custom_vjp
def low(v):
    return lax.optimization_barrier(v.astype(jnp.bfloat16)).astype(jnp.float32)

@jax.custom_vjp
def low_back(v):
    return v

def low_keep(v):
    return (low(v), None)

def low_pass(kept, grad):
    return (grad,)

def back_keep(v):
    return (v, None)

def back_low(kept, grad):
    return (low(grad),)
low.defvjp(low_keep, low_pass)
low_back.defvjp(back_keep, back_low)

def matmul(left, right):
    return jnp.dot(left, right, precision=lax.Precision.HIGHEST)

def layer_norm(values, gain_vec, shift_vec):
    average = lax.optimization_barrier(jnp.mean(values, axis=-1, keepdims=True))
    centered = values - average
    variance = lax.optimization_barrier(jnp.mean(centered * centered, axis=-1, keepdims=True))
    return centered * lax.rsqrt(variance + 1e-05) * gain_vec + shift_vec

def attend_whole(pieces):
    queries, key_rows, value_rows, usable = pieces
    scores = jnp.einsum('qhd,khd->hqk', queries, key_rows, precision=lax.Precision.HIGHEST) * DH ** (-0.5)
    scores = low_back(scores)
    scores = jnp.where(usable[None, None, :], scores, -1000000000.0)
    probabilities = jax.nn.softmax(scores, axis=-1)
    return jnp.einsum('hqk,khd->qhd', low(probabilities), value_rows, precision=lax.Precision.HIGHEST)

def make_forward(usable):

    def forward(speech, w_qkv, bias_query, bias_value, w_out, bias_out, gain_first, shift_first, w_up, bias_up, w_down, bias_down, gain_second, shift_second):
        token_rows = speech.reshape(-1, D)
        no_bias = jnp.zeros_like(bias_query)
        projected = matmul(token_rows, w_qkv) + jnp.concatenate([bias_query, no_bias, bias_value])
        projected = low(low_back(projected)).reshape(UTTS, FRAMES, 3, H, DH)
        attended = lax.map(jax.checkpoint(attend_whole), (projected[:, :, 0], projected[:, :, 1], projected[:, :, 2], usable))
        attended = low(low_back(attended.reshape(-1, D)))
        attn_out = low_back(matmul(attended, w_out) + bias_out)
        hidden = token_rows + attn_out
        normed = layer_norm(hidden, gain_first, shift_first)
        upward = low_back(matmul(low(normed), w_up) + bias_up)
        active = low(jax.nn.gelu(upward, approximate=False))
        branch = low_back(matmul(active, w_down) + bias_down)
        result = layer_norm(normed + branch, gain_second, shift_second)
        return result.reshape(UTTS, FRAMES, D)
    return forward

def reference(speech, lengths, grad_output, w_qkv, bias_query, bias_value, w_out, bias_out, gain_first, shift_first, w_up, bias_up, w_down, bias_down, gain_second, shift_second):
    usable = jnp.arange(FRAMES)[None, :] < lengths[:, None]
    inputs_f32 = tuple((item.astype(jnp.float32) for item in (speech, w_qkv, bias_query, bias_value, w_out, bias_out, gain_first, shift_first, w_up, bias_up, w_down, bias_down, gain_second, shift_second)))
    result, pullback = jax.vjp(make_forward(usable), *inputs_f32)
    gradients = pullback(grad_output.astype(jnp.float32))
    return (result.astype(jnp.bfloat16), gradients[0], gradients[1], gradients[2], gradients[3], gradients[4], gradients[5], gradients[6], gradients[7], gradients[8], gradients[9], gradients[10], gradients[11], gradients[12], gradients[13])
```

```python
import functools

import jax
import jax.numpy as jnp
from jax import lax
from jax.experimental import pallas as pl
from jax.experimental.pallas import tpu as pltpu
from jax.sharding import PartitionSpec as P

MESH = pl.DeviceIdType.MESH
VMEM = pltpu.VMEM
F32, BF16 = jnp.float32, jnp.bfloat16
H = 12
EPS = 1e-05
MASKED = -1000000000.0
NN = (((1,), (0,)), ((), ()))
NT = (((1,), (1,)), ((), ()))
ANY = pl.BlockSpec(memory_space=pl.ANY)
VM = pl.BlockSpec(memory_space=pltpu.VMEM)


def dot(a, b, dims=NN):
    return lax.dot_general(a, b, dims, preferred_element_type=F32)


def low(v):
    return v.astype(BF16)


def split3(v):
    hi = low(v)
    rest = v - hi.astype(F32)
    mid = low(rest)
    return hi.astype(F32), mid.astype(F32), rest - mid.astype(F32)


def place():
    dp = lax.axis_index("dp")
    return dp, lax.axis_index("blk"), lax.rem(dp, 2)


def lane_of(shape):
    return lax.broadcasted_iota(jnp.int32, shape, len(shape) - 1)


def attend_kernel(geo, x_ref, g_ref, lens_ref, w_hbm, b_ref,
                  xm, gm, qa, kall, vall, kb, o_ref,
                  w_ref, lens, q_scr, wsem, sx, rx, sg, rg, skv, rkv, sl):
    nb, hp, blk_len, d = geo
    dp, z, c = place()
    base = dp - c
    peer = (base + 1 - c, z)
    pairs = d // 128
    rows = nb * hp
    wcopy = pltpu.make_async_copy(w_hbm, w_ref, wsem)
    wcopy.start()

    barrier = pltpu.get_barrier_semaphore()
    for dz in range(nb):
        for dc in range(2):
            if dz or dc:
                pl.semaphore_signal(barrier, inc=1, device_id=(base + lax.rem(c + dc, 2), lax.rem(z + dz, nb)),
                                    device_id_type=MESH)
    pl.semaphore_wait(barrier, 2 * nb - 1)

    lens[c] = lens_ref[...]
    lcopy = pltpu.make_async_remote_copy(src_ref=lens_ref, dst_ref=lens.at[c], send_sem=sl.at[0], recv_sem=sl.at[1],
                                         device_id=peer, device_id_type=MESH)
    lcopy.start()

    def pieces(src, dst, ss, rs, start):
        for s in range(2):
            for h in range(2):
                to = 2 * c + s
                here = jnp.logical_and(to == z, c == h)
                part = src.at[s, pl.ds(h * hp, hp)]
                remote = pltpu.make_async_remote_copy(
                    src_ref=part, dst_ref=dst.at[z], send_sem=ss.at[2 * s + h], recv_sem=rs.at[z],
                    device_id=(base + h, to), device_id_type=MESH)

                @pl.when(jnp.logical_not(here))
                def _():
                    remote.start() if start else remote.wait_send()

                if start:
                    @pl.when(here)
                    def _():
                        pltpu.make_async_copy(part, dst.at[z], rs.at[z]).start()

    def arrive(src, dst, rs):
        for i in range(nb):
            pltpu.make_async_copy(src.at[0, pl.ds(0, hp)], dst.at[i], rs.at[i]).wait()

    pieces(x_ref, xm, sx, rx, True)
    wcopy.wait()
    arrive(x_ref, xm, rx)
    pieces(g_ref, gm, sg, rg, True)

    x = xm[...].reshape(rows, d)
    for part, scr in ((1, kall), (2, vall)):
        for p in range(pairs // 2):
            at = part * d + 256 * p
            t = low(dot(x, w_ref[:, at:at + 256]) + b_ref[:, at:at + 256])
            for e in range(2):
                scr[2 * p + e, c] = t[:, 128 * e:128 * e + 128]
    kvs = []
    for n, scr in enumerate((kall, vall)):
        kv = pltpu.make_async_remote_copy(src_ref=scr.at[:, c], dst_ref=scr.at[:, c], send_sem=skv.at[n],
                                          recv_sem=rkv.at[n], device_id=peer, device_id_type=MESH)
        kv.start()
        kvs.append(kv)
    for p in range(pairs // 2):
        at = 256 * p
        t = low(low(dot(x, w_ref[:, at:at + 256]) + b_ref[:, at:at + 256]).astype(F32) * 0.125)
        for e in range(2):
            q_scr[2 * p + e] = t[:, 128 * e:128 * e + 128]

    lcopy.wait()
    usable_len = lens[pl.ds(lax.div(z, 2), 1), pl.ds(lax.rem(z, 2), 1)].reshape(8, 128)[0:1]
    for h in range(2):
        for b in range(nb):
            t = lax.broadcasted_iota(jnp.int32, (hp, 128), 0) + h * hp
            frame = (t + blk_len * b).astype(F32)
            ok = jnp.logical_and(t < blk_len, frame < usable_len)
            kb[pl.ds((h * nb + b) * hp, hp), :] = low(jnp.where(ok, 0.0, MASKED))
    for kv in kvs:
        kv.wait()

    lane1 = lane_of((1, 128))
    lane_q = lane_of((rows, 128))

    def pair_step(p, _):
        kp = kall[p].reshape(2 * rows, 128)
        vp = vall[p].reshape(2 * rows, 128)
        qp = q_scr[p]
        bias = kb[...]
        outs = []
        for e in range(2):
            aux = 64 if e == 0 else 0
            own = (lane1 < 64) if e == 0 else (lane1 >= 64)
            own_m = low(own.astype(F32))
            first = low((lane1 == aux).astype(F32))
            ka = kp * own_m + bias * first
            va = vp * own_m + first
            qx = qp * own_m + first
            s = dot(qx, ka, NT)
            m = jnp.max(s, axis=1, keepdims=True)
            w = low(jnp.exp(s - m))
            oa = dot(w, va)
            total = oa[:, aux:aux + 1]
            outs.append(oa * (1.0 / total))
            hi, mid, lo = split3(m + jnp.log(total))
            tail = jnp.where(lane_q == aux, 1.0, jnp.where(lane_q == aux + 1, -hi, jnp.where(
                lane_q == aux + 2, -mid, jnp.where(lane_q == aux + 3, -lo, 0.0))))
            qa[2 * p + e] = qp * own_m + low(tail)
        o_ref[p] = jnp.where(lane_q < 64, outs[0], outs[1])
        return 0

    lax.fori_loop(0, pairs, pair_step, 0)

    arrive(g_ref, gm, rg)
    pieces(x_ref, xm, sx, rx, False)
    pieces(g_ref, gm, sg, rg, False)


def attend(x, g, lens, w_qkv, b_qkv, nb, hp, blk_len):
    d = x.shape[-1]
    rows = nb * hp
    pairs = d // 128
    out = [
        jax.ShapeDtypeStruct((nb, hp, d), BF16),
        jax.ShapeDtypeStruct((nb, hp, d), BF16),
        jax.ShapeDtypeStruct((H, rows, 128), BF16),
        jax.ShapeDtypeStruct((pairs, 2, rows, 128), BF16),
        jax.ShapeDtypeStruct((pairs, 2, rows, 128), BF16),
        jax.ShapeDtypeStruct((2 * rows, 128), BF16),
        jax.ShapeDtypeStruct((pairs, rows, 128), F32),
    ]
    dma = pltpu.SemaphoreType.DMA
    return pl.pallas_call(
        functools.partial(attend_kernel, (nb, hp, blk_len, d)),
        name="attend",
        out_shape=out,
        in_specs=[VM, VM, VM, ANY, VM],
        out_specs=[VM] * len(out),
        scratch_shapes=[
            VMEM(w_qkv.shape, BF16),
            VMEM((2, 2, 8, 128), F32),
            VMEM((pairs, rows, 128), BF16),
            dma, dma((4,)), dma((nb,)), dma((4,)), dma((nb,)), dma((2,)), dma((2,)), dma((2,)),
        ],
        compiler_params=pltpu.CompilerParams(collective_id=0, has_side_effects=True, vmem_limit_bytes=60 << 20),
    )(x, g, lens, w_qkv, b_qkv)
def norm(v, gain, shift):
    mean = jnp.mean(v, axis=1, keepdims=True)
    cen = v - mean
    inv = lax.rsqrt(jnp.mean(cen * cen, axis=1, keepdims=True) + EPS)
    n = cen * inv
    return n * gain + shift, n, inv


def norm_back(up, n, inv, gain):
    s = up * gain
    return inv * (s - jnp.mean(s, axis=1, keepdims=True) - n * jnp.mean(s * n, axis=1, keepdims=True))


def total(v):
    return jnp.sum(v, axis=0, keepdims=True)


FC = 512


def rows_kernel(xm, gm, o_ref, vec, bup, wo_hbm, wu_hbm, wd_hbm,
                out_ref, gh_ref, da_ref, gvec, gbup, gwo_ref, gwu_hbm, gwd_hbm,
                wo, wu, wd, ab, act, fac, n1_s, gs2, acc, stage_u, stage_d, sems, osem):
    rows, d = n1_s.shape
    chunks = act.shape[0]
    pairs = d // 128
    cw = pltpu.make_async_copy(wo_hbm, wo, sems.at[0])
    cu = pltpu.make_async_copy(wu_hbm, wu, sems.at[1])
    cd = pltpu.make_async_copy(wd_hbm, wd, sems.at[2])
    cw.start()
    cu.start()
    cd.start()
    bias_out, gain1, shift1, bias_down, gain2, shift2 = (vec[i:i + 1, :] for i in range(6))
    for p in range(pairs):
        ab[:, 128 * p:128 * p + 128] = low(o_ref[p])
    x = xm[...].reshape(rows, d).astype(F32)
    cw.wait()
    hidden = x + dot(ab[...], wo[...]) + bias_out
    normed, n1, inv1 = norm(hidden, gain1, shift1)
    n1_s[...] = n1
    acc[...] = normed + bias_down
    nl = low(normed)
    cu.wait()
    cd.wait()

    def up_step(j, _):
        at = pl.ds(pl.multiple_of(j * FC, FC), FC)
        u = dot(nl, wu[:, at]) + bup[:, at]
        cdf = 0.5 + 0.5 * lax.erf(u * 0.7071067811865476)
        dens = jnp.exp(-0.5 * u * u) * 0.3989422804014327
        a = low(u * cdf)
        act[j] = a
        fac[j] = cdf + u * dens
        acc[...] += dot(a, wd[at, :])
        return 0

    lax.fori_loop(0, chunks, up_step, 0)
    result, n2, inv2 = norm(acc[...], gain2, shift2)
    out_ref[...] = low(result).reshape(out_ref.shape)
    g = gm[...].reshape(rows, d).astype(F32)
    gvec[0:1, :] = total(g * n2)
    gvec[1:2, :] = total(g)
    back2 = norm_back(g, n2, inv2, gain2)
    gs2[...] = back2
    gb = low(back2)
    gvec[2:3, :] = total(gb.astype(F32))
    gbt = gb.T
    nt = nl.T

    acc[...] = back2

    def down_step(j, _):
        at = pl.ds(pl.multiple_of(j * FC, FC), FC)
        ga = dot(gb, wd[at, :], NT)
        gu32 = ga * fac[j]
        gu = low(gu32)
        gbup[:, at] = total(gu.astype(F32))
        acc[...] += dot(gu, wu[:, at], NT)
        stage_d[j] = low(dot(gbt, act[j]))
        stage_u[j] = low(dot(nt, gu))
        pltpu.make_async_copy(stage_d.at[j], gwd_hbm.at[:, at], osem.at[0, j]).start()
        pltpu.make_async_copy(stage_u.at[j], gwu_hbm.at[:, at], osem.at[1, j]).start()
        return 0

    lax.fori_loop(0, chunks, down_step, 0)
    gn = acc[...]
    n1 = n1_s[...]
    gvec[3:4, :] = total(gn * n1)
    gvec[4:5, :] = total(gn)
    gh = norm_back(gn, n1, inv1, gain1)
    gh_ref[...] = gh
    ga = low(gh)
    gvec[5:6, :] = total(ga.astype(F32))
    gvec[6:8, :] = jnp.zeros((2, d), F32)
    at = low(ab[...])
    gwo_ref[...] = low(dot(at.T, ga))
    datt = low(dot(ga, wo[...], NT))
    lane = lane_of((rows, 128))
    for p in range(pairs):
        dp_ = datt[:, 128 * p:128 * p + 128]
        prod = dp_.astype(F32) * o_ref[p]
        for e in range(2):
            aux = 64 if e == 0 else 0
            own = (lane < 64) if e == 0 else (lane >= 64)
            dd = jnp.sum(jnp.where(own, prod, 0.0), axis=1, keepdims=True)
            hi, mid, lo = split3(dd)
            tail = jnp.where(lane == aux, -hi, jnp.where(lane == aux + 1, -mid, jnp.where(lane == aux + 2, -lo, 0.0)))
            da_ref[2 * p + e] = low(jnp.where(own, dp_.astype(F32), tail))
    for j in range(chunks):
        at = pl.ds(j * FC, FC)
        pltpu.make_async_copy(stage_d.at[j], gwd_hbm.at[:, at], osem.at[0, j]).wait()
        pltpu.make_async_copy(stage_u.at[j], gwu_hbm.at[:, at], osem.at[1, j]).wait()


def rows_pass(xm, gm, o, vec, bup, w_out, w_up, w_down):
    nb, hp, d = xm.shape
    rows = nb * hp
    ff = w_up.shape[1]
    chunks = ff // FC
    out = [
        jax.ShapeDtypeStruct((nb, hp, d), BF16),
        jax.ShapeDtypeStruct((rows, d), F32),
        jax.ShapeDtypeStruct((H, rows, 128), BF16),
        jax.ShapeDtypeStruct((8, d), F32),
        jax.ShapeDtypeStruct((1, ff), F32),
        jax.ShapeDtypeStruct((d, d), BF16),
        jax.ShapeDtypeStruct((d, ff), BF16),
        jax.ShapeDtypeStruct((d, ff), BF16),
    ]
    dma = pltpu.SemaphoreType.DMA
    return pl.pallas_call(
        rows_kernel,
        name="rows_pass",
        out_shape=out,
        in_specs=[VM] * 5 + [ANY] * 3,
        out_specs=[VM] * 6 + [ANY] * 2,
        scratch_shapes=[
            VMEM(w_out.shape, BF16), VMEM(w_up.shape, BF16), VMEM(w_down.shape, BF16),
            VMEM((rows, d), BF16), VMEM((chunks, rows, FC), BF16), VMEM((chunks, rows, FC), F32),
            VMEM((rows, d), F32), VMEM((rows, d), F32), VMEM((rows, d), F32),
            VMEM((chunks, d, FC), BF16), VMEM((chunks, d, FC), BF16),
            dma((3,)), dma((2, chunks)),
        ],
        compiler_params=pltpu.CompilerParams(vmem_limit_bytes=60 << 20),
    )(xm, gm, o, vec, bup, w_out, w_up, w_down)
def bit_of(v, k):
    return lax.rem(lax.div(v, 1 << k), 2)


def flip(v, k):
    return v + (1 << k) - (2 << k) * bit_of(v, k)


class Sum:
    def __init__(self, where, order, src, part, own, r0, r1, r2, rx, zs, rz, sems, piece, own_ready=None):
        self.dp, self.z, self.nbits, self.nb = where
        self.order, self.src, self.part = order, src, part
        self.own, self.r0, self.r1, self.r2, self.rx, self.zs, self.rz = own, r0, r1, r2, rx, zs, rz
        self.sems, self.piece = sems, piece
        low_bit = self.nbits - 3
        self.bits = [low_bit + k for k in order]
        self.mine = [bit_of(self.dp, t) for t in self.bits]
        self.extra = list(range(low_bit))

    def remote(self, src, dst, n, to):
        return pltpu.make_async_remote_copy(src_ref=src, dst_ref=dst, send_sem=self.sems.at[0, n],
                                            recv_sem=self.sems.at[1, n], device_id=to, device_id_type=MESH)

    def index(self, first, a, b):
        k0, k1, k2 = self.order
        return (first << k0) + (a << k1) + (b << k2) if not isinstance(first, int) else None

    def part_at(self, m0, a, b):
        k0, k1, k2 = self.order
        return m0 * (1 << k0) + a * (1 << k1) + b * (1 << k2)

    def copies(self, stage):
        to = (flip(self.dp, self.bits[stage]), self.z)
        m = self.mine
        if stage == 0:
            return [self.remote(self.part(self.src, self.part_at(1 - m[0], a, b)), self.r0.at[a, b], 2 * a + b, to)
                    for a in range(2) for b in range(2)]
        if stage == 1:
            return [self.remote(self.r0.at[1 - m[1]], self.r1, 4, to)]
        return [self.remote(self.r0.at[m[1], 1 - m[2]], self.r2, 5, to)]

    def local(self):
        m = self.mine
        return [pltpu.make_async_copy(self.part(self.src, self.part_at(m[0], a, b)), self.own.at[a, b],
                                      self.sems.at[0, 8 + 2 * a + b]) for a in range(2) for b in range(2)]

    def start(self):
        for c in self.copies(0):
            c.start()
        for c in self.local():
            c.start()

    def next1(self):
        for c in self.local():
            c.wait()
        for c in self.copies(0):
            c.wait()
        m1 = self.mine[1]
        self.r0[1 - m1] = self.r0[1 - m1] + self.own[1 - m1]
        for c in self.copies(1):
            c.start()
        self.r0[m1] = self.r0[m1] + self.own[m1]

    def next2(self):
        for c in self.copies(1):
            c.wait()
        m1, m2 = self.mine[1:]
        self.r0[m1, 1 - m2] = self.r0[m1, 1 - m2] + self.r1[1 - m2]
        for c in self.copies(2):
            c.start()
        self.r0[m1, m2] = self.r0[m1, m2] + self.r1[m2]

    def pieces(self):
        out = []
        for dz in range(1, self.nb):
            to = lax.rem(self.z + dz, self.nb)
            out.append(self.remote(self.zs.at[to], self.rz.at[self.z], 12 + dz, (self.dp, to)))
        return out

    def landed(self):
        for dz in range(1, self.nb):
            frm = lax.rem(self.z + self.nb - dz, self.nb)
            self.remote(self.zs.at[frm], self.rz.at[frm], 12 + dz, (self.dp, frm)).wait_recv()

    def next3(self):
        for c in self.copies(2):
            c.wait()
        m1, m2 = self.mine[1:]
        v = self.r0[m1, m2].astype(F32) + self.r2[...].astype(F32)
        for n, t in enumerate(self.extra):
            self.r2[...] = low(v)
            c = self.remote(self.r2, self.rx.at[n], 16 + n, (flip(self.dp, t), self.z))
            c.start()
            c.wait()
            v = v + self.rx[n].astype(F32)
        self.piece(self.zs, low(v))
        for c in self.pieces():
            c.start()

    def finish(self):
        self.landed()
        for c in self.pieces():
            c.wait_send()
        v = self.zs[self.z].astype(F32)
        for dz in range(1, self.nb):
            v = v + self.rz[lax.rem(self.z + dz, self.nb)].astype(F32)
        return v


def grads_kernel(geo, xm, om, qa, kall, vall, kb, da, gh, gvec, gbup, gwo, wq_hbm, gwd_hbm, gwu_hbm,
                 out_z, dx_z, fd, fu, fq, fv,
                 wq, gq, dqkv, kvown, kvsend, kvrecv, dxs,
                 owd, r0d, r1d, r2d, rxd, zsd, rzd,
                 owu, r0u, r1u, r2u, rxu, zsu, rzu,
                 r0a, r1a, r2a, rxa, zsa, rza,
                 r0b, r1b, r2b, rxb, zsb, rzb,
                 rv, wsem, sd, su, sa, sb, so, ro, sx, rx, skv, rkv, sv):
    nb, hp, nbits = geo
    dp, z, c = place()
    base = dp - c
    peer = (base + 1 - c, z)
    rows, d = gh.shape
    pairs = d // 128
    wcopy = pltpu.make_async_copy(wq_hbm, wq, wsem)
    wcopy.start()

    barrier = pltpu.get_barrier_semaphore()
    count = 0
    for dz in range(nb):
        for dc in range(2):
            if dz or dc:
                pl.semaphore_signal(barrier, inc=1, device_id=(base + lax.rem(c + dc, 2), lax.rem(z + dz, nb)),
                                    device_id_type=MESH)
                count += 1
    for t in range(1, nbits):
        pl.semaphore_signal(barrier, inc=1, device_id=(flip(dp, t), z), device_id_type=MESH)
        count += 1
    pl.semaphore_wait(barrier, count)

    def back(src, dst, ss, rs, start):
        for b in range(nb):
            to_c = lax.div(z, 2)
            here = jnp.logical_and(z == b, c == to_c)
            land = dst.at[lax.rem(z, 2), pl.ds(pl.multiple_of(c * hp, 16), hp)]
            n = 2 * lax.rem(z, 2) + c
            remote = pltpu.make_async_remote_copy(src_ref=src.at[b], dst_ref=land, send_sem=ss.at[b],
                                                  recv_sem=rs.at[n], device_id=(base + to_c, jnp.int32(b)),
                                                  device_id_type=MESH)

            @pl.when(jnp.logical_not(here))
            def _():
                remote.start() if start else remote.wait_send()

            if start:
                @pl.when(here)
                def _():
                    pltpu.make_async_copy(src.at[b], land, rs.at[n]).start()

    def arrive(src, dst, rs):
        for n in range(4):
            pltpu.make_async_copy(src.at[0], dst.at[n // 2, pl.ds((n % 2) * hp, hp)], rs.at[n]).wait()

    where = (dp, z, nbits, nb)
    part_r = d // 8
    part_f = gwd_hbm.shape[1] // 8
    row_part = lambda ref, p: ref.at[pl.ds(pl.multiple_of(p * part_r, 16), part_r), :]
    col_part = lambda ref, p: ref.at[:, pl.ds(pl.multiple_of(p * part_f, 128), part_f)]

    def row_pieces(zs, v):
        n = v.shape[0] // nb
        for j in range(nb):
            zs[j] = v[n * j:n * j + n, :]

    def col_pieces(zs, v):
        n = v.shape[1] // nb
        for j in range(nb):
            zs[j] = v[:, n * j:n * j + n]

    def whole(zs, v):
        zs[0] = v

    jd = Sum(where, (0, 1, 2), gwd_hbm, col_part, owd, r0d, r1d, r2d, rxd, zsd, rzd, sd, row_pieces)
    ju = Sum(where, (0, 2, 1), gwu_hbm, row_part, owu, r0u, r1u, r2u, rxu, zsu, rzu, su, col_pieces)
    jd.start()
    ju.start()
    back(om, out_z, so, ro, True)

    gq[:, 3 * d:4 * d] = gwo[...]
    lane1 = lane_of((1, 128))
    lane = lane_of((rows, 128))

    def kvcopy(p):
        return pltpu.make_async_remote_copy(src_ref=kvsend.at[p], dst_ref=kvrecv.at[p], send_sem=skv.at[p],
                                            recv_sem=rkv.at[p], device_id=peer, device_id_type=MESH)

    def pair_step(p, _):
        @pl.when(p == 1)
        def _():
            jd.next1()
            ju.next1()

        @pl.when(p == pairs - 1)
        def _():
            jd.next2()
            ju.next2()

        dq = [None, None]
        for n in range(2):
            h = (1 - c) if n == 0 else c
            kp = kall[p, h]
            vp = vall[p, h]
            bias = kb[pl.ds(pl.multiple_of(h * rows, 16), rows), :]
            kt = kp.T
            dks, dvs = [], []
            for e in range(2):
                aux = 64 if e == 0 else 0
                own = (lane1 < 64) if e == 0 else (lane1 >= 64)
                own_m = low(own.astype(F32))
                first = low((lane1 == aux).astype(F32))
                ones = lambda lo, hi: low(jnp.logical_and(lane1 >= aux + lo, lane1 <= aux + hi).astype(F32))
                kx = kp * own_m + (bias * first + ones(1, 3))
                vx = vp * own_m + ones(0, 2)
                q = qa[2 * p + e]
                do = da[2 * p + e]
                pt = jnp.exp(dot(kx, q, NT))
                ds = low(pt * dot(vx, do, NT))
                dvs.append(dot(low(pt), do))
                dks.append(dot(ds, q))
                t = dot(kt[64 * e:64 * e + 64, :], ds)
                dq[e] = t if dq[e] is None else dq[e] + t
            dk = jnp.where(lane < 64, dks[0], dks[1])
            dv = jnp.where(lane < 64, dvs[0], dvs[1])
            if n == 0:
                kvsend[p, 0] = low(dk)
                kvsend[p, 1] = low(dv)
                kvcopy(p).start()
            else:
                kvown[p, 0] = dk
                kvown[p, 1] = dv
        dqp = jnp.concatenate(dq, axis=0).T * 0.125
        dqkv[:, pl.ds(pl.multiple_of(p * 128, 128), 128)] = low(dqp)
        return 0

    lax.fori_loop(0, pairs, pair_step, 0)
    for p in range(pairs):
        kvcopy(p).wait()
        for n in range(2):
            at = (n + 1) * d + 128 * p
            dqkv[:, at:at + 128] = low(kvown[p, n] + kvrecv[p, n].astype(F32))

    xt = xm[...].reshape(rows, d).T
    for j in range(3 * d // 256):
        gq[:, 256 * j:256 * j + 256] = low(dot(xt, dqkv[:, 256 * j:256 * j + 256]))
    half = gq.shape[1] // 2
    row_part_a = lambda ref, p: ref.at[pl.ds(pl.multiple_of(p * part_r, 16), part_r), pl.ds(0, half)]
    row_part_b = lambda ref, p: ref.at[pl.ds(pl.multiple_of(p * part_r, 16), part_r), pl.ds(half, half)]

    class Held(Sum):
        def local(self):
            return []

        def add(self, at):
            self.r0[at] = self.r0[at]

        def next1(self):
            for cc in self.copies(0):
                cc.wait()
            m = self.mine

            def grow(a):
                for b in range(2):
                    own = self.part(self.src, self.part_at(m[0], a, b))
                    self.r0[a, b] = self.r0[a, b] + own[...]
            grow(1 - m[1])
            for cc in self.copies(1):
                cc.start()
            grow(m[1])

    ja = Held(where, (0, 1, 2), gq, row_part_a, None, r0a, r1a, r2a, rxa, None, None, sa, None)
    jb = Held(where, (0, 2, 1), gq, row_part_b, None, r0b, r1b, r2b, rxb, None, None, sb, None)
    ja.start()
    jb.start()

    vec = fv
    vec[0:8, :] = gvec[...]
    for i in range(gbup.shape[1] // d):
        vec[8 + i:9 + i, :] = gbup[:, d * i:d * i + d]
    vec[12:13, :] = total(dqkv[:, 0:d].astype(F32))
    vec[13:14, :] = total(dqkv[:, 2 * d:3 * d].astype(F32))
    vec[14:16, :] = jnp.zeros((2, d), F32)

    wcopy.wait()
    dx = low(gh[...] + dot(dqkv[...], wq[...], NT))
    dxs[...] = dx.reshape(dxs.shape)
    back(dxs, dx_z, sx, rx, True)

    jd.next3()
    ju.next3()
    ja.next1()
    jb.next1()

    steps = [((flip(dp, t), z), t) for t in range(nbits)] + [((dp, flip(z, t)), nbits + t) for t in range(2)]
    for to, n in steps:
        cp = pltpu.make_async_remote_copy(src_ref=vec, dst_ref=rv.at[n], send_sem=sv.at[0, n], recv_sem=sv.at[1, n],
                                          device_id=to, device_id_type=MESH)
        cp.start()
        cp.wait()
        vec[...] += rv[n]

    ja.next2()
    jb.next2()
    fd[...] = jd.finish()
    fu[...] = ju.finish()

    def last(job):
        for cc in job.copies(2):
            cc.wait()
        m1, m2 = job.mine[1:]
        v = job.r0[m1, m2].astype(F32) + job.r2[...].astype(F32)
        for n, t in enumerate(job.extra):
            job.r2[...] = low(v)
            cp = job.remote(job.r2, job.rx.at[n], 16 + n, (flip(dp, t), z))
            cp.start()
            cp.wait()
            v = v + job.rx[n].astype(F32)
        return v

    va, vb = last(ja), last(jb)
    v = jnp.concatenate([va, vb], axis=1)

    def cut(zs, v):
        wq_, wo_ = 3 * d // nb, d // nb
        rolled = pltpu.roll(v, v.shape[1] - 64, 1)
        for j in range(nb):
            at = 0
            for first, w in ((0, wq_), (3 * d, wo_)):
                s0 = first + w * j
                r = s0 % 128
                wide = -(-w // 128) * 128
                zs[j, :, at:at + wide] = low((rolled if r else v)[:, s0 - r:s0 - r + wide])
                at += wide
    jz = Sum(where, (0, 1, 2), None, None, None, None, None, None, None, zsa, rza, sa, None)
    cut(zsa, v)
    for cc in jz.pieces():
        cc.start()
    fq[...] = jz.finish()

    back(om, out_z, so, ro, False)
    arrive(om, out_z, ro)
    back(dxs, dx_z, sx, rx, False)
    arrive(dxs, dx_z, rx)


def grads(nbits, xm, om, qa, kall, vall, kb, da, gh, gvec, gbup, gwo, w_qkv, gwd, gwu):
    nb, hp, d = xm.shape
    rows = nb * hp
    pairs = d // 128
    ff = gwd.shape[1]
    pr, pf = d // 8, ff // 8
    wide = -(-(3 * d // nb) // 128) * 128 + -(-(d // nb) // 128) * 128
    extra = max(nbits - 3, 1)
    out = [
        jax.ShapeDtypeStruct((2, 2 * hp, d), BF16),
        jax.ShapeDtypeStruct((2, 2 * hp, d), BF16),
        jax.ShapeDtypeStruct((d // nb, pf), F32),
        jax.ShapeDtypeStruct((pr, ff // nb), F32),
        jax.ShapeDtypeStruct((pr, wide), F32),
        jax.ShapeDtypeStruct((16, d), F32),
    ]
    dma = pltpu.SemaphoreType.DMA

    def job(r, c, own, pieces):
        got = [VMEM((2, 2, r, c), BF16)] if own else []
        got += [VMEM((2, 2, r, c), BF16), VMEM((2, r, c), BF16), VMEM((r, c), BF16), VMEM((extra, r, c), BF16)]
        return got + [VMEM((nb,) + pieces, BF16)] * 2
    scratch = [
        VMEM(w_qkv.shape, BF16), VMEM((d, 4 * d), BF16), VMEM((rows, 3 * d), BF16),
        VMEM((pairs, 2, rows, 128), F32), VMEM((pairs, 2, rows, 128), BF16), VMEM((pairs, 2, rows, 128), BF16),
        VMEM((nb, hp, d), BF16),
    ]
    scratch += job(d, pf, True, (d // nb, pf)) + job(pr, ff, True, (pr, ff // nb))
    scratch += job(pr, 2 * d, False, (pr, wide)) + job(pr, 2 * d, False, (8, 128))
    scratch += [VMEM((nbits + 2, 16, d), F32), dma] + [dma((2, 16 + extra))] * 4
    scratch += [dma((nb,)), dma((4,)), dma((nb,)), dma((4,)), dma((pairs,)), dma((pairs,)), dma((2, nbits + 2))]
    return pl.pallas_call(
        functools.partial(grads_kernel, (nb, hp, nbits)),
        name="grads",
        out_shape=out,
        in_specs=[VM] * 11 + [ANY] * 3,
        out_specs=[VM] * len(out),
        scratch_shapes=scratch,
        compiler_params=pltpu.CompilerParams(collective_id=1, has_side_effects=True, vmem_limit_bytes=60 << 20),
    )(xm, om, qa, kall, vall, kb, da, gh, gvec, gbup, gwo, w_qkv, gwd, gwu)
def shards(speech, lengths, grad_output, w_qkv, bias_query, bias_value, w_out, bias_out, gain_first, shift_first,
           w_up, bias_up, w_down, bias_down, gain_second, shift_second):
    utts, blk_len, d = speech.shape
    nb = lax.axis_size("blk")
    ndp = lax.axis_size("dp")
    nbits = ndp.bit_length() - 1
    hp = -(-blk_len // 32) * 16
    fill = ((0, 0), (0, 2 * hp - blk_len), (0, 0))
    lens = jnp.broadcast_to(lengths.astype(F32)[:, None, None], (utts, 8, 128))
    b_qkv = jnp.concatenate([bias_query, jnp.zeros_like(bias_query), bias_value])[None]
    vec = jnp.stack([bias_out, gain_first, shift_first, bias_down, gain_second, shift_second])
    xm, gm, qa, kall, vall, kb, o = attend(jnp.pad(speech, fill), jnp.pad(grad_output, fill), lens, w_qkv, b_qkv,
                                           nb, hp, blk_len)
    om, gh, da, gvec, gbup, gwo, gwu, gwd = rows_pass(xm, gm, o, vec, bias_up[None], w_out, w_up, w_down)
    out_z, dx_z, fd, fu, fq, fv = grads(nbits, xm, om, qa, kall, vall, kb, da, gh, gvec, gbup, gwo, w_qkv, gwd, gwu)
    dp = lax.axis_index("dp")
    parts = ndp // 8
    sub = lax.rem(dp, parts)

    def mine(v, axis):
        if parts == 1:
            return v
        n = v.shape[axis] // parts
        return lax.dynamic_slice_in_dim(v, sub * n, n, axis)

    wq, wo = 3 * d // nb, d // nb
    at = -(-wq // 128) * 128
    ff = bias_up.shape[0]
    return (
        out_z[:, :blk_len],
        dx_z[:, :blk_len].astype(F32),
        mine(fq[:, :wq], 0),
        fv[12],
        fv[13],
        mine(fq[:, at:at + wo], 0),
        fv[5],
        fv[3],
        fv[4],
        mine(fu, 0),
        fv[8:8 + ff // d].reshape(ff),
        mine(fd.T, 0),
        fv[2],
        fv[0],
        fv[1],
    )


def solution(mesh):
    rows = P("dp", "blk", None)
    cut = P("dp", "blk")
    return jax.shard_map(
        shards,
        mesh=mesh,
        in_specs=(rows, P("dp"), rows) + (P(),) * 13,
        out_specs=(rows, rows, cut, P(), P(), cut, P(), P(), P(), cut, P(), cut, P(), P(), P()),
        check_vma=False,
    )
```

```python
import functools

import jax
import jax.numpy as jnp
from jax import lax
from jax.experimental import pallas as pl
from jax.experimental.pallas import tpu as pltpu
from jax.sharding import PartitionSpec as P

MESH = pl.DeviceIdType.MESH
VMEM = pltpu.VMEM
F32, BF16 = jnp.float32, jnp.bfloat16
EPS = 1e-05
MASKED = -1000000000.0
FC = 512
NN = (((1,), (0,)), ((), ()))
NT = (((1,), (1,)), ((), ()))
ANY = pl.BlockSpec(memory_space=pl.ANY)
VM = pl.BlockSpec(memory_space=pltpu.VMEM)


def dot(a, b, dims=NN):
    return lax.dot_general(a, b, dims, preferred_element_type=F32)


def low(v):
    return v.astype(BF16)


def total(v):
    return jnp.sum(v, axis=0, keepdims=True)


def split3(v):
    hi = low(v)
    rest = v - hi.astype(F32)
    mid = low(rest)
    return hi.astype(F32), mid.astype(F32), rest - mid.astype(F32)


def lane_of(shape):
    return lax.broadcasted_iota(jnp.int32, shape, len(shape) - 1)


def bit_of(v, k):
    return lax.rem(lax.div(v, 1 << k), 2)


def flip(v, k):
    return v + (1 << k) - (2 << k) * bit_of(v, k)


def norm(v, gain, shift):
    mean = jnp.mean(v, axis=1, keepdims=True)
    cen = v - mean
    inv = lax.rsqrt(jnp.mean(cen * cen, axis=1, keepdims=True) + EPS)
    n = cen * inv
    return n * gain + shift, n, inv


def norm_back(up, n, inv, gain):
    s = up * gain
    return inv * (s - jnp.mean(s, axis=1, keepdims=True) - n * jnp.mean(s * n, axis=1, keepdims=True))


def link(src, dst, sems, n, to):
    return pltpu.make_async_remote_copy(src_ref=src, dst_ref=dst, send_sem=sems.at[0, n], recv_sem=sems.at[1, n],
                                        device_id=to, device_id_type=MESH)


class Halving:
    def __init__(self, dp, z, nbits, order, part, r0, r1, r2, sems):
        self.dp, self.z, self.order, self.part = dp, z, order, part
        self.r0, self.r1, self.r2, self.sems = r0, r1, r2, sems
        self.bits = [nbits - 3 + k for k in order]
        self.mine = [bit_of(dp, t) for t in self.bits]

    def at(self, m, a, b):
        k0, k1, k2 = self.order
        return self.part(m * (1 << k0) + a * (1 << k1) + b * (1 << k2))

    def copies(self, stage):
        to = (flip(self.dp, self.bits[stage]), self.z)
        m = self.mine
        if stage == 0:
            return [link(self.at(1 - m[0], a, b), self.r0.at[a, b], self.sems, 2 * a + b, to)
                    for a in range(2) for b in range(2)]
        if stage == 1:
            return [link(self.r0.at[1 - m[1]], self.r1, self.sems, 4, to)]
        return [link(self.r0.at[m[1], 1 - m[2]], self.r2, self.sems, 5, to)]

    def start(self):
        for c in self.copies(0):
            c.start()

    def next1(self):
        for c in self.copies(0):
            c.wait()
        m = self.mine
        for a in (1 - m[1], m[1]):
            for b in range(2):
                self.r0[a, b] = self.r0[a, b] + self.at(m[0], a, b)[...]
            if a is not m[1]:
                for c in self.copies(1):
                    c.start()

    def next2(self):
        for c in self.copies(1):
            c.wait()
        m1, m2 = self.mine[1:]
        self.r0[m1, 1 - m2] = self.r0[m1, 1 - m2] + self.r1[1 - m2]
        for c in self.copies(2):
            c.start()
        self.r0[m1, m2] = self.r0[m1, m2] + self.r1[m2]

    def result(self):
        for c in self.copies(2):
            c.wait()
        return self.r0[self.mine[1], self.mine[2]].astype(F32) + self.r2[...].astype(F32)


class Pieces:
    def __init__(self, dp, z, nbits, zs, r1, r2, rx, sems):
        self.zs, self.r1, self.r2, self.rx, self.sems = zs, r1, r2, rx, sems
        self.more = [(flip(dp, t), z) for t in range(nbits - 3)]
        self.b = [bit_of(z, 0), bit_of(z, 1)]
        self.to = [(dp, flip(z, 0)), (dp, flip(z, 1))]

    def first(self):
        return link(self.zs.at[1 - self.b[0]], self.r1, self.sems, 0, self.to[0])

    def second(self):
        return link(self.zs.at[self.b[0], 1 - self.b[1]], self.r2, self.sems, 1, self.to[1])

    def start(self):
        self.first().start()

    def next1(self):
        self.first().wait()
        b0, b1 = self.b
        self.zs[b0, 1 - b1] = self.zs[b0, 1 - b1] + self.r1[1 - b1]
        self.second().start()

    def result(self):
        self.second().wait()
        b0, b1 = self.b
        v = self.zs[b0, b1].astype(F32) + self.r1[b1].astype(F32) + self.r2[...].astype(F32)
        for n, to in enumerate(self.more):
            self.zs[b0, b1] = low(v)
            c = link(self.zs.at[b0, b1], self.rx.at[n], self.sems, 2 + n, to)
            c.start()
            c.wait()
            v = v + self.rx[n].astype(F32)
        return v


def layer_kernel(geo, len_ref, x_ref, g_ref, bq, bv, bo, g1, s1, bu, bd, g2, s2, wq_hbm, wo_hbm, wu_hbm, wd_hbm,
                 out_z, dx_z, fd, fu, fq, fv, *scratch):
    nb, hp, nbits, heads = geo
    (wq, wo, wu, wd, xm, gm, om, qa, kall, vall, kb, o_s, ab, nl, inv1, act, fac, n1_s, acc, gwd, gwu, kvrecv, lens, rv, vhalf, rv2, vec2,
     *rest) = scratch
    jobs, rest = rest[:24], rest[24:]
    zbufs, (wsem, lsem, kvsem, kvs2, vsem, vsem2, sx, rx, sg, rg, so, ro, sd, rd, *jsem) = rest[:12], rest[12:]
    blk_len, d = x_ref.shape[1:]
    dp, z = lax.axis_index("dp"), lax.axis_index("blk")
    c = lax.rem(dp, 2)
    base = dp - c
    peer = (base + 1 - c, z)
    rows, ff = act.shape
    nq = (1 << nbits) // 2
    pairs = d // 128
    chunks = ff // FC
    gq = wu
    da = fac
    dqkv = act
    dxs = gm

    weights = [pltpu.make_async_copy(a, b, wsem.at[n])
               for n, (a, b) in enumerate(((wq_hbm, wq), (wo_hbm, wo), (wu_hbm, wu), (wd_hbm, wd)))]
    weights[0].start()

    barrier = pltpu.get_barrier_semaphore()
    greet = [(base + lax.rem(c + dc, 2), lax.rem(z + dz, nb)) for dz in range(nb) for dc in range(2) if dz or dc]
    greet += [(lax.rem(lax.div(dp, 2) + n, nq) * 2 + c, z) for n in range(1, nq)]
    for to in greet:
        pl.semaphore_signal(barrier, inc=1, device_id=to, device_id_type=MESH)

    for src, dst in ((x_ref, out_z), (g_ref, dx_z)):
        for s in range(2):
            dst[s, 2 * hp - 16:, :] = jnp.zeros((16, d), BF16)
            dst[s, 0:blk_len, :] = src[s]
    for s in range(2):
        lens[c, s] = jnp.full((8, 128), len_ref[s], jnp.int32).astype(F32)
    pl.semaphore_wait(barrier, len(greet))

    lcopy = pltpu.make_async_remote_copy(src_ref=lens.at[c], dst_ref=lens.at[c], send_sem=lsem.at[0],
                                         recv_sem=lsem.at[1], device_id=peer, device_id_type=MESH)

    def spread(src, dst, ss, rs, start):
        for s in range(2):
            for h in range(2):
                to = 2 * c + s
                here = jnp.logical_and(to == z, c == h)
                part = src.at[s, pl.ds(h * hp, hp)]
                remote = pltpu.make_async_remote_copy(
                    src_ref=part, dst_ref=dst.at[z], send_sem=ss.at[2 * s + h], recv_sem=rs.at[z],
                    device_id=(base + h, to), device_id_type=MESH)

                @pl.when(jnp.logical_not(here))
                def _():
                    remote.start() if start else remote.wait_send()

                if start:
                    @pl.when(here)
                    def _():
                        pltpu.make_async_copy(part, dst.at[z], rs.at[z]).start()

    def spread_in(src, dst, rs):
        for i in range(nb):
            pltpu.make_async_copy(src.at[0, pl.ds(0, hp)], dst.at[i], rs.at[i]).wait()

    def back(src, dst, ss, rs, start):
        for b in range(nb):
            to_c = lax.div(z, 2)
            here = jnp.logical_and(z == b, c == to_c)
            land = dst.at[lax.rem(z, 2), pl.ds(pl.multiple_of(c * hp, 16), hp)]
            n = 2 * lax.rem(z, 2) + c
            remote = pltpu.make_async_remote_copy(src_ref=src.at[b], dst_ref=land, send_sem=ss.at[b],
                                                  recv_sem=rs.at[n], device_id=(base + to_c, jnp.int32(b)),
                                                  device_id_type=MESH)

            @pl.when(jnp.logical_not(here))
            def _():
                remote.start() if start else remote.wait_send()

            if start:
                @pl.when(here)
                def _():
                    pltpu.make_async_copy(src.at[b], land, rs.at[n]).start()

    def back_in(src, dst, rs):
        for n in range(4):
            pltpu.make_async_copy(src.at[0], dst.at[n // 2, pl.ds((n % 2) * hp, hp)], rs.at[n]).wait()

    lane1 = lane_of((1, 128))
    lane = lane_of((rows, 128))
    own = [lane1 < 64, lane1 >= 64]
    own_m = [low(o.astype(F32)) for o in own]
    auxes = (64, 0)

    def at_aux(e, lo, hi):
        return low(jnp.logical_and(lane1 >= auxes[e] + lo, lane1 <= auxes[e] + hi).astype(F32))

    row = lambda ref: ref[...].reshape(1, ref.shape[0])

    spread(out_z, xm, sx, rx, True)
    lcopy.start()
    weights[0].wait()
    for w in weights[1:]:
        w.start()
    spread_in(out_z, xm, rx)
    spread(out_z, xm, sx, rx, False)
    spread(dx_z, gm, sg, rg, True)
    x = xm[...].reshape(rows, d)
    kvs = []
    for part, scr in ((1, kall), (2, vall)):
        for p in range(pairs // 2):
            at = part * d + 256 * p
            t = dot(x, wq[:, at:at + 256])
            if part == 2:
                t = t + row(bv)[:, 256 * p:256 * p + 256]
            t = low(t)
            for e in range(2):
                scr[2 * p + e, c] = t[:, 128 * e:128 * e + 128]
        kv = pltpu.make_async_remote_copy(src_ref=scr.at[:, c], dst_ref=scr.at[:, c], send_sem=kvs2.at[0, part - 1],
                                          recv_sem=kvs2.at[1, part - 1], device_id=peer, device_id_type=MESH)
        kv.start()
        kvs.append(kv)
    for p in range(pairs // 2):
        at = 256 * p
        t = low(dot(x, wq[:, at:at + 256]) + row(bq)[:, at:at + 256])
        t = low(t.astype(F32) * 0.125)
        for q in range(2):
            for e in range(2):
                qa[2 * (2 * p + q) + e] = t[:, 128 * q:128 * q + 128] * own_m[e] + at_aux(e, 0, 0)
    lcopy.wait()
    usable_len = lens[lax.div(z, 2), lax.rem(z, 2)][0:1]
    for h in range(2):
        for b in range(nb):
            t = lax.broadcasted_iota(jnp.int32, (hp, 128), 0) + h * hp
            frame = (t + blk_len * b).astype(F32)
            ok = jnp.logical_and(t < blk_len, frame < usable_len)
            kb[pl.ds((h * nb + b) * hp, hp), :] = low(jnp.where(ok, 0.0, MASKED))
    for kv in kvs:
        kv.wait()

    def attend_step(p, _):
        kp = kall[p].reshape(2 * rows, 128)
        vp = vall[p].reshape(2 * rows, 128)
        bias = kb[...]
        outs = []
        for e in range(2):
            aux = auxes[e]
            first = at_aux(e, 0, 0)
            ka = kp * own_m[e] + bias * first
            va = vp * own_m[e] + first
            qx = qa[2 * p + e]
            s = dot(qx, ka, NT)
            m = jnp.max(s, axis=1, keepdims=True)
            oa = dot(low(jnp.exp(s - m)), va)
            tot = oa[:, aux:aux + 1]
            outs.append(oa * (1.0 / tot))
            hi, mid, lo = split3(m + jnp.log(tot))
            tail = jnp.where(lane == aux + 1, -hi, jnp.where(lane == aux + 2, -mid, jnp.where(lane == aux + 3, -lo, 0.0)))
            qa[2 * p + e] = qx + low(tail)
        o_s[p] = jnp.where(lane < 64, outs[0], outs[1])
        return 0

    lax.fori_loop(0, pairs, attend_step, 0)

    for p in range(pairs):
        ab[:, 128 * p:128 * p + 128] = low(o_s[p])
    weights[1].wait()
    acc[...] = dot(ab[...], wo[...])

    def norm1(i, _):
        at = pl.ds(pl.multiple_of(i * hp, 16), hp)
        normed, n, inv = norm(xm[i].astype(F32) + acc[at] + row(bo), row(g1), row(s1))
        n1_s[at] = n
        inv1[at] = jnp.broadcast_to(inv, (hp, 128))
        acc[at] = normed + row(bd)
        nl[at] = low(normed)
        return 0

    lax.fori_loop(0, nb, norm1, 0)
    weights[2].wait()
    weights[3].wait()

    for j in range(chunks):
        at = slice(j * FC, j * FC + FC)
        u = dot(nl[...], wu[:, at]) + row(bu)[:, at]
        cdf = 0.5 + 0.5 * lax.erf(u * 0.7071067811865476)
        dens = jnp.exp(-0.5 * u * u) * 0.3989422804014327
        a = low(u * cdf)
        act[:, at] = a
        fac[:, at] = low(cdf + u * dens)
        acc[...] += dot(a, wd[at, :])
    spread_in(dx_z, gm, rg)
    spread(dx_z, gm, sg, rg, False)
    fv[...] = jnp.zeros(fv.shape, F32)

    def norm2(i, _):
        at = pl.ds(pl.multiple_of(i * hp, 16), hp)
        result, n2, inv2 = norm(acc[at], row(g2), row(s2))
        om[i] = low(result)
        g = gm[i].astype(F32)
        fv[0:1, :] += total(g * n2)
        fv[1:2, :] += total(g)
        back2 = norm_back(g, n2, inv2, row(g2))
        acc[at] = back2
        gb = low(back2)
        fv[2:3, :] += total(gb.astype(F32))
        gm[i] = gb
        return 0

    lax.fori_loop(0, nb, norm2, 0)
    back(om, out_z, so, ro, True)
    gb = gm[...].reshape(rows, d)
    gbt = gb.T

    def make(n, order, part):
        return Halving(dp, z, nbits, order, part, *jobs[3 * n:3 * n + 3], jsem[n])

    pr, pf = d // 8, ff // 8
    hd, hf = d // 2, ff // 2
    rows_of = lambda ref, p, at, n: ref.at[pl.ds(pl.multiple_of(p * pr, 16), pr), pl.ds(at, n)]
    def down_part(i, p):
        if i == 0:
            return gwd.at[:, pl.ds(pl.multiple_of(p * pf, 128), pf)]
        across = wq.shape[1] // pf
        return wq.at[pl.ds(pl.multiple_of(lax.div(p, across) * hd, 16), hd),
                     pl.ds(pl.multiple_of(lax.rem(p, across) * pf, 128), pf)]

    jd = [make(i, ((0, 1, 2), (0, 2, 1))[i], functools.partial(down_part, i)) for i in range(2)]
    ju = [make(2 + i, ((0, 1, 2), (0, 2, 1))[i], functools.partial(
        lambda i, p: rows_of(gwu, p, i * hf, hf), i)) for i in range(2)]
    for i in range(2):
        for p in range(0, 8, 2):
            t = low(dot(gbt[i * hd:i * hd + hd, :], act[:, p * pf:p * pf + 2 * pf]))
            down_part(i, p)[...] = t[:, :pf]
            down_part(i, p + 1)[...] = t[:, pf:]
        jd[i].start()

    nt = nl[...].T
    for j in range(chunks):
        at = slice(j * FC, j * FC + FC)
        gu = low(dot(gb, wd[at, :], NT) * fac[:, at].astype(F32))
        bup = total(gu.astype(F32))
        for i in range(FC // 128):
            k = j * FC + 128 * i
            fv[8 + k // d:9 + k // d, k % d:k % d + 128] = bup[:, 128 * i:128 * i + 128]
        acc[...] += dot(gu, wu[:, at], NT)
        gwu[:, at] = low(dot(nt, gu))
        if j == 1:
            jd[0].next1()
        if j == 2:
            jd[1].next1()
            ju[0].start()
    ju[1].start()

    def norm1_back(i, _):
        at = pl.ds(pl.multiple_of(i * hp, 16), hp)
        gn = acc[at]
        n1 = n1_s[at]
        fv[3:4, :] += total(gn * n1)
        fv[4:5, :] += total(gn)
        gh = norm_back(gn, n1, inv1[at, 0:1], row(g1))
        n1_s[at] = gh
        ga = low(gh)
        fv[5:6, :] += total(ga.astype(F32))
        nl[at] = ga
        return 0

    lax.fori_loop(0, nb, norm1_back, 0)
    ga = nl[...]
    datt = low(dot(ga, wo[...], NT))
    for p in range(pairs):
        dop = datt[:, 128 * p:128 * p + 128]
        prod = dop.astype(F32) * o_s[p]
        for e in range(2):
            aux = auxes[e]
            hi, mid, lo = split3(jnp.sum(jnp.where(own[e], prod, 0.0), axis=1, keepdims=True))
            tail = jnp.where(lane == aux, -hi, jnp.where(lane == aux + 1, -mid, jnp.where(lane == aux + 2, -lo, 0.0)))
            k = 128 * (2 * p + e)
            da[:, k:k + 128] = dop * own_m[e] + low(tail)
    at_ = ab[...].T
    q3 = 3 * d
    hq = q3 // 2
    gwo = low(dot(at_, ga))
    gq[:, hq:hq + hd] = gwo[:, :hd]
    gq[:, 2 * hq + hd:2 * hq + 2 * hd] = gwo[:, hd:]

    plane = [((lax.rem(lax.div(dp, 2) + n, nq) * 2 + c), z) for n in range(1, nq)]
    column = [(dp, lax.rem(z + n, nb)) for n in range(1, nb)]

    def exchange(src, got, sems, first, to, start):
        for n, t in enumerate(to):
            cp = link(src, got.at[first + n], sems, first + n, t)
            cp.start() if start else cp.wait()
        if not start:
            v = src[...]
            for n in range(len(to)):
                v = v + got[first + n]
            src[...] = v

    def vec_step(n):
        mine = pl.ds(pl.multiple_of(8 * c, 8), 8)
        other = pl.ds(pl.multiple_of(8 - 8 * c, 8), 8)
        halves = link(fv.at[other], rv.at[0], vsem, 0, peer)
        back_ = link(vhalf, fv.at[mine], vsem, nq + nb - 1, peer)
        if n == 0:
            halves.start()
        elif n == 1:
            halves.wait()
            vhalf[...] = fv[mine] + rv[0]
            exchange(vhalf, rv, vsem, 1, plane, True)
        elif n == 2:
            exchange(vhalf, rv, vsem, 1, plane, False)
            exchange(vhalf, rv, vsem, nq, column, True)
        elif n == 3:
            exchange(vhalf, rv, vsem, nq, column, False)
            back_.start()
        else:
            back_.wait()
            fv[mine] = vhalf[...]

    def vec2_step(n):
        groups = [(0, [peer]), (1, plane), (nq, column)]
        if n > 0:
            exchange(vec2, rv2, vsem2, *groups[n - 1], False)
        if n < 3:
            exchange(vec2, rv2, vsem2, *groups[n], True)

    def kvcopy(p):
        src = wd.at[pl.ds(pl.multiple_of(p * 512, 16), rows), pl.ds(0, 256)]
        return pltpu.make_async_remote_copy(src_ref=src, dst_ref=kvrecv.at[p], send_sem=kvsem.at[0, p],
                                            recv_sem=kvsem.at[1, p], device_id=peer, device_id_type=MESH)

    def pair_step(p, _):
        dq = [None, None]
        for n in range(2):
            h = (1 - c) if n == 0 else c
            kp = kall[p, h]
            vp = vall[p, h]
            bias = kb[pl.ds(pl.multiple_of(h * rows, 16), rows), :]
            kt = kp.T
            dks, dvs = [], []
            for e in range(2):
                kx = kp * own_m[e] + (bias * at_aux(e, 0, 0) + at_aux(e, 1, 3))
                vx = vp * own_m[e] + at_aux(e, 0, 2)
                q = qa[2 * p + e]
                do = da[:, pl.ds(pl.multiple_of((2 * p + e) * 128, 128), 128)]
                pt = jnp.exp(dot(kx, q, NT))
                ds = low(pt * dot(vx, do, NT))
                dvs.append(dot(low(pt), do))
                dks.append(dot(ds, q))
                t = dot(kt[64 * e:64 * e + 64, :], ds)
                dq[e] = t if dq[e] is None else dq[e] + t
            dk = jnp.where(lane < 64, dks[0], dks[1])
            dv = jnp.where(lane < 64, dvs[0], dvs[1])
            if n == 0:
                at = pl.ds(pl.multiple_of(p * 512, 16), rows)
                wd[at, 0:128] = low(dk)
                wd[at, 128:256] = low(dv)
                kvcopy(p).start()
            else:
                o_s[p] = dk
                acc[:, pl.ds(pl.multiple_of(p * 128, 128), 128)] = dv
        dqp = jnp.concatenate(dq, axis=0).T * 0.125
        dqkv[:, pl.ds(pl.multiple_of(p * 128, 128), 128)] = low(dqp)
        return 0

    part_q = [(0, 2 * hd), (2 * hd, hq + hd)]
    jq = []
    for t in range(2):
        for i in range(2):
            at0 = t * (hq + hd) + i * 2 * hd
            jq.append(make(4 + 2 * t + i, ((0, 1, 2), (0, 2, 1))[i], functools.partial(
                lambda at0, p: rows_of(gq, p, at0, 2 * hd), at0)))
    half = pairs // 2

    def finish_pairs(t):
        for p in range(t * half, t * half + half):
            kvcopy(p).wait()
            dqkv[:, d + 128 * p:d + 128 * p + 128] = low(o_s[p] + kvrecv[p, :, 0:128].astype(F32))
            dqkv[:, 2 * d + 128 * p:2 * d + 128 * p + 128] = low(
                acc[:, 128 * p:128 * p + 128] + kvrecv[p, :, 128:256].astype(F32))
        xt = xm[...].reshape(rows, d).T
        for n in range(3):
            at = t * (hq + hd) + n * hd
            gq[:, at:at + hd] = low(dot(xt, dqkv[:, n * d + t * hd:n * d + t * hd + hd]))
            if n == 1:
                jq[2 * t].start()
        jq[2 * t + 1].start()

    zd = Pieces(dp, z, nbits, *zbufs[0:4], jsem[8])
    zu = Pieces(dp, z, nbits, *zbufs[4:8], jsem[9])
    zq = Pieces(dp, z, nbits, *zbufs[8:12], jsem[10])

    pr_z = d // nb

    def at_p(k, what):
        def f(p):
            @pl.when(p == k)
            def _():
                what()
        return f

    def step1():
        vec_step(1)

    def step2():
        jd[0].next2()
        jd[1].next2()
        ju[0].next1()
        ju[1].next1()

    def step3():
        finish_pairs(0)
        vec_step(2)

    def step4():
        vd = jnp.concatenate([jd[0].result(), jd[1].result()], axis=0)
        for j in range(nb):
            zd.zs[j % 2, j // 2] = low(vd[pr_z * j:pr_z * j + pr_z, :])
        zd.start()
        weights[0].start()

    def step5():
        jq[0].next1()
        jq[1].next1()
        vec_step(3)

    vec_step(0)
    todo = [at_p(1, step1), at_p(2, step2), at_p(3, step3), at_p(4, step4), at_p(5, step5)]

    def step(p, carry):
        for t in todo:
            t(p)
        return pair_step(p, carry)

    lax.fori_loop(0, pairs, step, 0)
    finish_pairs(1)
    weights[0].wait()
    for n in range(3):
        n1_s[...] += dot(dqkv[:, n * d:n * d + d], wq[:, n * d:n * d + d], NT)
    dx = low(n1_s[...])
    dxs[...] = dx.reshape(dxs.shape)
    zd.next1()
    vec_step(4)
    back(dxs, dx_z, sd, rd, True)
    third = d // 3
    for n, k in ((0, 0), (1, 2 * d)):
        t = total(dqkv[:, k:k + d].astype(F32))
        for i in range(3):
            vec2[3 * n + i:3 * n + i + 1, :] = t[:, third * i:third * i + third]
    vec2[6:8, :] = jnp.zeros((2, third), F32)
    vec2_step(0)
    ju[0].next2()
    ju[1].next2()
    jq[2].next1()
    jq[3].next1()
    vec2_step(1)
    jq[0].next2()
    jq[1].next2()
    vec2_step(2)
    vu = [ju[0].result(), ju[1].result()]
    n = ff // nb
    for j in range(nb):
        k = j * n
        zu.zs[j % 2, j // 2] = low(vu[k // hf][:, k % hf:k % hf + n])
    zu.start()
    fd[...] = zd.result()
    jq[2].next2()
    jq[3].next2()
    zu.next1()
    vec2_step(3)
    for n in range(2):
        for i in range(3):
            fv[12 + n:13 + n, third * i:third * i + third] = vec2[3 * n + i:3 * n + i + 1, :]
    va = [jq[0].result(), jq[1].result()]
    vb = [jq[2].result(), jq[3].result()]
    cols = []
    for n, (i, k) in enumerate(((0, 0), (0, 1), (1, 0), (1, 1))):
        cols += [va[i][:, k * hd:k * hd + hd], vb[i][:, k * hd:k * hd + hd]]
    v = jnp.concatenate(cols, axis=1)
    rolled = pltpu.roll(v, v.shape[1] - 64, 1)
    for j in range(nb):
        at = 0
        for first, w in ((0, q3 // nb), (q3, d // nb)):
            s0 = first + w * j
            r = s0 % 128
            wide = -(-w // 128) * 128
            zq.zs[j % 2, j // 2, :, at:at + wide] = low((rolled if r else v)[:, s0 - r:s0 - r + wide])
            at += wide
    zq.start()
    fu[...] = zu.result()
    back(om, out_z, so, ro, False)
    back_in(om, out_z, ro)
    zq.next1()
    back(dxs, dx_z, sd, rd, False)
    back_in(dxs, dx_z, rd)
    fq[...] = zq.result()


def layer(nbits, nb, lengths, speech, grad_output, vectors, w_qkv, w_out, w_up, w_down):
    blk_len, d = speech.shape[1:]
    hp = -(-blk_len // 32) * 16
    heads = d // 64
    rows = nb * hp
    pairs = d // 128
    ff = w_up.shape[1]
    pr, pf = d // 8, ff // 8
    wide = -(-(3 * d // nb) // 128) * 128 + -(-(d // nb) // 128) * 128
    extra = nbits - 3
    nq = (1 << nbits) // 2
    out = [
        jax.ShapeDtypeStruct((2, 2 * hp, d), BF16),
        jax.ShapeDtypeStruct((2, 2 * hp, d), BF16),
        jax.ShapeDtypeStruct((d // nb, pf), F32),
        jax.ShapeDtypeStruct((pr, ff // nb), F32),
        jax.ShapeDtypeStruct((pr, wide), F32),
        jax.ShapeDtypeStruct((16, d), F32),
    ]
    dma = pltpu.SemaphoreType.DMA

    def job(r, c):
        return [VMEM((2, 2, r, c), BF16), VMEM((2, r, c), BF16), VMEM((r, c), BF16)]

    def pieces(r, c):
        more = (extra, r, c) if extra else (8, 128)
        return [VMEM((2, 2, r, c), BF16), VMEM((2, r, c), BF16), VMEM((r, c), BF16), VMEM(more, BF16)]

    scratch = [
        VMEM(w_qkv.shape, BF16), VMEM(w_out.shape, BF16), VMEM(w_up.shape, BF16), VMEM(w_down.shape, BF16),
        VMEM((nb, hp, d), BF16), VMEM((nb, hp, d), BF16), VMEM((nb, hp, d), BF16),
        VMEM((heads, rows, 128), BF16), VMEM((pairs, 2, rows, 128), BF16), VMEM((pairs, 2, rows, 128), BF16),
        VMEM((2 * rows, 128), BF16), VMEM((pairs, rows, 128), F32), VMEM((rows, d), BF16),
        VMEM((rows, d), BF16), VMEM((rows, 128), F32),
        VMEM((rows, ff), BF16), VMEM((rows, ff), BF16),
        VMEM((rows, d), F32), VMEM((rows, d), F32),
        VMEM((d // 2, ff), BF16), VMEM((d, ff), BF16), VMEM((pairs, rows, 256), BF16),
        VMEM((2, 2, 8, 128), F32), VMEM((nq + nb - 1, 8, d), F32), VMEM((8, d), F32),
        VMEM((nq + nb - 1, 8, d // 3), F32), VMEM((8, d // 3), F32),
    ]
    scratch += job(d // 2, pf) * 2 + job(pr, ff // 2) * 2 + job(pr, d) * 4
    scratch += pieces(d // nb, pf) + pieces(pr, ff // nb) + pieces(pr, wide)
    scratch += [dma((4,)), dma((2,)), dma((2, pairs)), dma((2, 2)), dma((2, nq + nb)), dma((2, nq + nb - 1))]
    scratch += [dma((4,))] * 8
    scratch += [dma((2, 6))] * 8 + [dma((2, 2 + extra))] * 3
    return pl.pallas_call(
        functools.partial(layer_kernel, (nb, hp, nbits, heads)),
        name="layer",
        out_shape=out,
        in_specs=[pl.BlockSpec(memory_space=pltpu.SMEM)] + [VM] * 11 + [ANY] * 4,
        out_specs=[VM] * len(out),
        scratch_shapes=scratch,
        compiler_params=pltpu.CompilerParams(collective_id=0, has_side_effects=True, vmem_limit_bytes=64 << 20),
    )(lengths, speech, grad_output, *vectors, w_qkv, w_out, w_up, w_down)


def finish_kernel(blk_len, cols, out_z, dx_z, fd, fu, fq, fv, out, dx, gq, bq, bv, go, bo, g1, s1, gu, bu, gd, bd, g2, s2):
    wq, wo, at = cols
    d = dx.shape[2]
    out[...] = out_z[:, :blk_len]
    dx[...] = dx_z[:, :blk_len].astype(F32)
    gq[...] = fq[:, :wq]
    go[...] = fq[:, at:at + wo]
    gu[...] = fu[...]
    gd[...] = fd[...]
    for ref, n in ((g2, 0), (s2, 1), (bd, 2), (g1, 3), (s1, 4), (bo, 5), (bq, 12), (bv, 13)):
        ref[...] = fv[n:n + 1, :].reshape(d)
    for n in range(bu.shape[0] // d):
        bu[d * n:d * n + d] = fv[8 + n:9 + n, :].reshape(d)


def shards(speech, lengths, grad_output, w_qkv, bias_query, bias_value, w_out, bias_out, gain_first, shift_first,
           w_up, bias_up, w_down, bias_down, gain_second, shift_second):
    utts, blk_len, d = speech.shape
    nb = lax.axis_size("blk")
    ndp = lax.axis_size("dp")
    nbits = ndp.bit_length() - 1
    ff = bias_up.shape[0]
    vectors = (bias_query, bias_value, bias_out, gain_first, shift_first, bias_up, bias_down, gain_second, shift_second)
    got = layer(nbits, nb, lengths, speech, grad_output, vectors, w_qkv, w_out, w_up, w_down)
    wq, wo = 3 * d // nb, d // nb
    at = -(-wq // 128) * 128
    shape = jax.ShapeDtypeStruct
    vec = shape((d,), F32)
    res = pl.pallas_call(
        functools.partial(finish_kernel, blk_len, (wq, wo, at)),
        name="finish",
        out_shape=[
            shape((utts, blk_len, d), BF16), shape((utts, blk_len, d), F32), shape((d // 8, wq), F32), vec, vec,
            shape((d // 8, wo), F32), vec, vec, vec, shape((d // 8, ff // nb), F32), shape((ff,), F32),
            shape((wo, ff // 8), F32), vec, vec, vec,
        ],
        in_specs=[VM] * 6,
        out_specs=[VM] * 15,
        compiler_params=pltpu.CompilerParams(vmem_limit_bytes=60 << 20),
    )(*got)
    res = list(res)
    res[11] = res[11].T
    parts = ndp // 8
    if parts > 1:
        sub = lax.rem(lax.axis_index("dp"), parts)
        for i in (2, 5, 9, 11):
            n = res[i].shape[0] // parts
            res[i] = lax.dynamic_slice_in_dim(res[i], sub * n, n, 0)
    return tuple(res)


def solution(mesh):
    rows = P("dp", "blk", None)
    cut = P("dp", "blk")
    return jax.shard_map(
        shards,
        mesh=mesh,
        in_specs=(rows, P("dp"), rows) + (P(),) * 13,
        out_specs=(rows, rows, cut, P(), P(), cut, P(), P(), P(), cut, P(), cut, P(), P(), P()),
        check_vma=False,
    )
```

```python
import functools

import jax
import jax.numpy as jnp
from jax import lax
from jax.experimental import pallas as pl
from jax.experimental.pallas import tpu as pltpu
from jax.sharding import PartitionSpec as P

MESH = pl.DeviceIdType.MESH
VMEM = pltpu.VMEM
F32, BF16 = jnp.float32, jnp.bfloat16
EPS = 1e-05
MASKED = -1000000000.0
FC = 512
NN = (((1,), (0,)), ((), ()))
NT = (((1,), (1,)), ((), ()))
ANY = pl.BlockSpec(memory_space=pl.ANY)
VM = pl.BlockSpec(memory_space=pltpu.VMEM)


def dot(a, b, dims=NN):
    return lax.dot_general(a, b, dims, preferred_element_type=F32)


def low(v):
    return v.astype(BF16)


def total(v):
    return jnp.sum(v, axis=0, keepdims=True)


def split3(v):
    hi = low(v)
    rest = v - hi.astype(F32)
    mid = low(rest)
    return hi.astype(F32), mid.astype(F32), rest - mid.astype(F32)


def lane_of(shape):
    return lax.broadcasted_iota(jnp.int32, shape, len(shape) - 1)


def bit_of(v, k):
    return lax.rem(lax.div(v, 1 << k), 2)


def flip(v, k):
    return v + (1 << k) - (2 << k) * bit_of(v, k)


def norm(v, gain, shift):
    mean = jnp.mean(v, axis=1, keepdims=True)
    cen = v - mean
    inv = lax.rsqrt(jnp.mean(cen * cen, axis=1, keepdims=True) + EPS)
    n = cen * inv
    return n * gain + shift, n, inv


def norm_back(up, n, inv, gain):
    s = up * gain
    return inv * (s - jnp.mean(s, axis=1, keepdims=True) - n * jnp.mean(s * n, axis=1, keepdims=True))


def link(src, dst, sems, n, to):
    return pltpu.make_async_remote_copy(src_ref=src, dst_ref=dst, send_sem=sems.at[0, n], recv_sem=sems.at[1, n],
                                        device_id=to, device_id_type=MESH)


class Halving:
    def __init__(self, dp, z, nbits, order, part, r0, r1, r2, sems):
        self.dp, self.z, self.order, self.part = dp, z, order, part
        self.r0, self.r1, self.r2, self.sems = r0, r1, r2, sems
        self.bits = [nbits - 3 + k for k in order]
        self.mine = [bit_of(dp, t) for t in self.bits]

    def at(self, m, a, b):
        k0, k1, k2 = self.order
        return self.part(m * (1 << k0) + a * (1 << k1) + b * (1 << k2))

    def copies(self, stage):
        to = (flip(self.dp, self.bits[stage]), self.z)
        m = self.mine
        if stage == 0:
            return [link(self.at(1 - m[0], a, b), self.r0.at[a, b], self.sems, 2 * a + b, to)
                    for a in range(2) for b in range(2)]
        if stage == 1:
            return [link(self.r0.at[1 - m[1]], self.r1, self.sems, 4, to)]
        return [link(self.r0.at[m[1], 1 - m[2]], self.r2, self.sems, 5, to)]

    def start(self):
        for c in self.copies(0):
            c.start()

    def next1(self):
        for c in self.copies(0):
            c.wait()
        m = self.mine
        for a in (1 - m[1], m[1]):
            for b in range(2):
                self.r0[a, b] = self.r0[a, b] + self.at(m[0], a, b)[...]
            if a is not m[1]:
                for c in self.copies(1):
                    c.start()

    def next2(self):
        for c in self.copies(1):
            c.wait()
        m1, m2 = self.mine[1:]
        self.r0[m1, 1 - m2] = self.r0[m1, 1 - m2] + self.r1[1 - m2]
        for c in self.copies(2):
            c.start()
        self.r0[m1, m2] = self.r0[m1, m2] + self.r1[m2]

    def result(self):
        for c in self.copies(2):
            c.wait()
        return self.r0[self.mine[1], self.mine[2]].astype(F32) + self.r2[...].astype(F32)


class Pieces:
    def __init__(self, dp, z, nbits, zs, r1, r2, rx, sems):
        self.zs, self.r1, self.r2, self.rx, self.sems = zs, r1, r2, rx, sems
        self.more = [(flip(dp, t), z) for t in range(nbits - 3)]
        self.b = [bit_of(z, 0), bit_of(z, 1)]
        self.to = [(dp, flip(z, 0)), (dp, flip(z, 1))]

    def first(self):
        return link(self.zs.at[1 - self.b[0]], self.r1, self.sems, 0, self.to[0])

    def second(self):
        return link(self.zs.at[self.b[0], 1 - self.b[1]], self.r2, self.sems, 1, self.to[1])

    def start(self):
        self.first().start()

    def next1(self):
        self.first().wait()
        b0, b1 = self.b
        self.zs[b0, 1 - b1] = self.zs[b0, 1 - b1] + self.r1[1 - b1]
        self.second().start()

    def result(self):
        self.second().wait()
        b0, b1 = self.b
        v = self.zs[b0, b1].astype(F32) + self.r1[b1].astype(F32) + self.r2[...].astype(F32)
        for n, to in enumerate(self.more):
            self.zs[b0, b1] = low(v)
            c = link(self.zs.at[b0, b1], self.rx.at[n], self.sems, 2 + n, to)
            c.start()
            c.wait()
            v = v + self.rx[n].astype(F32)
        return v


def layer_kernel(geo, len_ref, x_ref, g_ref, bq, bv, bo, g1, s1, bu, bd, g2, s2, wq_hbm, wo_hbm, wu_hbm, wd_hbm,
                 out_z, dx_z, fd, fu, fq, fv, *scratch):
    nb, hp, nbits, heads = geo
    (wq, wo, wu, wd, xm, gm, om, qa, kall, vall, kb, o_s, ab, nl, inv1, act, fac, n1_s, acc, gwd, gwu, kvrecv, lens, rv, vhalf, rv2, vec2,
     *rest) = scratch
    jobs, rest = rest[:24], rest[24:]
    zbufs, (wsem, lsem, kvsem, kvs2, vsem, vsem2, sx, rx, sg, rg, so, ro, sd, rd, *jsem) = rest[:16], rest[16:]
    blk_len, d = x_ref.shape[1:]
    dp, z = lax.axis_index("dp"), lax.axis_index("blk")
    c = lax.rem(dp, 2)
    base = dp - c
    peer = (base + 1 - c, z)
    rows, ff = act.shape
    nq = (1 << nbits) // 2
    pairs = d // 128
    chunks = ff // FC
    gq = wu
    da = fac
    dqkv = act
    dxs = gm

    weights = [pltpu.make_async_copy(a, b, wsem.at[n])
               for n, (a, b) in enumerate(((wq_hbm, wq), (wo_hbm, wo), (wu_hbm, wu), (wd_hbm, wd)))]
    weights[0].start()

    barrier = pltpu.get_barrier_semaphore()
    greet = [(base + lax.rem(c + dc, 2), lax.rem(z + dz, nb)) for dz in range(nb) for dc in range(2) if dz or dc]
    greet += [(lax.rem(lax.div(dp, 2) + n, nq) * 2 + c, z) for n in range(1, nq)]
    for to in greet:
        pl.semaphore_signal(barrier, inc=1, device_id=to, device_id_type=MESH)

    for src, dst in ((x_ref, out_z), (g_ref, dx_z)):
        for s in range(2):
            dst[s, 2 * hp - 16:, :] = jnp.zeros((16, d), BF16)
            dst[s, 0:blk_len, :] = src[s]
    for s in range(2):
        lens[c, s] = jnp.full((8, 128), len_ref[s], jnp.int32).astype(F32)
    pl.semaphore_wait(barrier, len(greet))

    lcopy = pltpu.make_async_remote_copy(src_ref=lens.at[c], dst_ref=lens.at[c], send_sem=lsem.at[0],
                                         recv_sem=lsem.at[1], device_id=peer, device_id_type=MESH)

    def spread(src, dst, ss, rs, start):
        for s in range(2):
            for h in range(2):
                to = 2 * c + s
                here = jnp.logical_and(to == z, c == h)
                part = src.at[s, pl.ds(h * hp, hp)]
                remote = pltpu.make_async_remote_copy(
                    src_ref=part, dst_ref=dst.at[z], send_sem=ss.at[2 * s + h], recv_sem=rs.at[z],
                    device_id=(base + h, to), device_id_type=MESH)

                @pl.when(jnp.logical_not(here))
                def _():
                    remote.start() if start else remote.wait_send()

                if start:
                    @pl.when(here)
                    def _():
                        pltpu.make_async_copy(part, dst.at[z], rs.at[z]).start()

    def spread_in(src, dst, rs):
        for i in range(nb):
            pltpu.make_async_copy(src.at[0, pl.ds(0, hp)], dst.at[i], rs.at[i]).wait()

    def back(src, dst, ss, rs, start):
        for b in range(nb):
            to_c = lax.div(z, 2)
            here = jnp.logical_and(z == b, c == to_c)
            land = dst.at[lax.rem(z, 2), pl.ds(pl.multiple_of(c * hp, 16), hp)]
            n = 2 * lax.rem(z, 2) + c
            remote = pltpu.make_async_remote_copy(src_ref=src.at[b], dst_ref=land, send_sem=ss.at[b],
                                                  recv_sem=rs.at[n], device_id=(base + to_c, jnp.int32(b)),
                                                  device_id_type=MESH)

            @pl.when(jnp.logical_not(here))
            def _():
                remote.start() if start else remote.wait_send()

            if start:
                @pl.when(here)
                def _():
                    pltpu.make_async_copy(src.at[b], land, rs.at[n]).start()

    def back_in(src, dst, rs):
        for n in range(4):
            pltpu.make_async_copy(src.at[0], dst.at[n // 2, pl.ds((n % 2) * hp, hp)], rs.at[n]).wait()

    lane1 = lane_of((1, 128))
    lane = lane_of((rows, 128))
    own = [lane1 < 64, lane1 >= 64]
    own_m = [low(o.astype(F32)) for o in own]
    auxes = (64, 0)

    def at_aux(e, lo, hi):
        return low(jnp.logical_and(lane1 >= auxes[e] + lo, lane1 <= auxes[e] + hi).astype(F32))

    row = lambda ref: ref[...].reshape(1, ref.shape[0])

    spread(out_z, xm, sx, rx, True)
    lcopy.start()
    weights[0].wait()
    for w in weights[1:]:
        w.start()
    spread_in(out_z, xm, rx)
    spread(out_z, xm, sx, rx, False)
    spread(dx_z, gm, sg, rg, True)
    x = xm[...].reshape(rows, d)

    def kv_in(n, p):
        scr = (kall, vall)[n]
        return pltpu.make_async_remote_copy(src_ref=scr.at[p, c], dst_ref=scr.at[p, c], send_sem=kvs2.at[0, n, p],
                                            recv_sem=kvs2.at[1, n, p], device_id=peer, device_id_type=MESH)

    for p in range(pairs // 2):
        for n, scr in enumerate((kall, vall)):
            at = (n + 1) * d + 256 * p
            t = dot(x, wq[:, at:at + 256])
            if n == 1:
                t = t + row(bv)[:, 256 * p:256 * p + 256]
            t = low(t)
            for e in range(2):
                scr[2 * p + e, c] = t[:, 128 * e:128 * e + 128]
                kv_in(n, 2 * p + e).start()
    for p in range(pairs // 2):
        at = 256 * p
        t = low(dot(x, wq[:, at:at + 256]) + row(bq)[:, at:at + 256])
        t = low(t.astype(F32) * 0.125)
        for q in range(2):
            for e in range(2):
                qa[2 * (2 * p + q) + e] = t[:, 128 * q:128 * q + 128] * own_m[e] + at_aux(e, 0, 0)
    lcopy.wait()
    usable_len = lens[lax.div(z, 2), lax.rem(z, 2)][0:1]
    for h in range(2):
        for b in range(nb):
            t = lax.broadcasted_iota(jnp.int32, (hp, 128), 0) + h * hp
            frame = (t + blk_len * b).astype(F32)
            ok = jnp.logical_and(t < blk_len, frame < usable_len)
            kb[pl.ds((h * nb + b) * hp, hp), :] = low(jnp.where(ok, 0.0, MASKED))

    def attend_step(p, _):
        for n in range(2):
            kv_in(n, p).wait()
        kp = kall[p].reshape(2 * rows, 128)
        vp = vall[p].reshape(2 * rows, 128)
        bias = kb[...]
        outs = []
        for e in range(2):
            aux = auxes[e]
            first = at_aux(e, 0, 0)
            ka = kp * own_m[e] + bias * first
            va = vp * own_m[e] + first
            qx = qa[2 * p + e]
            s = dot(qx, ka, NT)
            m = jnp.max(s, axis=1, keepdims=True)
            oa = dot(low(jnp.exp(s - m)), va)
            tot = oa[:, aux:aux + 1]
            outs.append(oa * (1.0 / tot))
            hi, mid, lo = split3(m + jnp.log(tot))
            tail = jnp.where(lane == aux + 1, -hi, jnp.where(lane == aux + 2, -mid, jnp.where(lane == aux + 3, -lo, 0.0)))
            qa[2 * p + e] = qx + low(tail)
        o_s[p] = jnp.where(lane < 64, outs[0], outs[1])
        return 0

    lax.fori_loop(0, pairs, attend_step, 0, unroll=2)

    for p in range(pairs):
        ab[:, 128 * p:128 * p + 128] = low(o_s[p])
    weights[1].wait()
    acc[...] = dot(ab[...], wo[...])

    def norm1(i, _):
        at = pl.ds(pl.multiple_of(i * hp, 16), hp)
        normed, n, inv = norm(xm[i].astype(F32) + acc[at] + row(bo), row(g1), row(s1))
        n1_s[at] = n
        inv1[at] = jnp.broadcast_to(inv, (hp, 128))
        acc[at] = normed + row(bd)
        nl[at] = low(normed)
        return 0

    lax.fori_loop(0, nb, norm1, 0)
    weights[2].wait()
    weights[3].wait()

    for j in range(chunks):
        at = slice(j * FC, j * FC + FC)
        u = dot(nl[...], wu[:, at]) + row(bu)[:, at]
        cdf = 0.5 + 0.5 * lax.erf(u * 0.7071067811865476)
        dens = jnp.exp(-0.5 * u * u) * 0.3989422804014327
        a = low(u * cdf)
        act[:, at] = a
        fac[:, at] = low(cdf + u * dens)
        acc[...] += dot(a, wd[at, :])
    spread_in(dx_z, gm, rg)
    spread(dx_z, gm, sg, rg, False)
    fv[...] = jnp.zeros(fv.shape, F32)

    def norm2(i, _):
        at = pl.ds(pl.multiple_of(i * hp, 16), hp)
        result, n2, inv2 = norm(acc[at], row(g2), row(s2))
        om[i] = low(result)
        g = gm[i].astype(F32)
        fv[0:1, :] += total(g * n2)
        fv[1:2, :] += total(g)
        back2 = norm_back(g, n2, inv2, row(g2))
        acc[at] = back2
        gb = low(back2)
        fv[2:3, :] += total(gb.astype(F32))
        gm[i] = gb
        return 0

    lax.fori_loop(0, nb, norm2, 0)
    gb = gm[...].reshape(rows, d)
    gbt = gb.T

    def make(n, order, part):
        return Halving(dp, z, nbits, order, part, *jobs[3 * n:3 * n + 3], jsem[n])

    pr, pf = d // 8, ff // 8
    hd, hf = d // 2, ff // 2
    rows_of = lambda ref, p, at, n: ref.at[pl.ds(pl.multiple_of(p * pr, 16), pr), pl.ds(at, n)]
    def down_part(i, p):
        if i == 0:
            return gwd.at[:, pl.ds(pl.multiple_of(p * pf, 128), pf)]
        across = wq.shape[1] // pf
        return wq.at[pl.ds(pl.multiple_of(lax.div(p, across) * hd, 16), hd),
                     pl.ds(pl.multiple_of(lax.rem(p, across) * pf, 128), pf)]

    jd = [make(i, ((0, 1, 2), (0, 2, 1))[i], functools.partial(down_part, i)) for i in range(2)]
    ju = [make(2 + i, ((0, 2, 1), (0, 1, 2))[i], functools.partial(
        lambda i, p: rows_of(gwu, p, i * hf, hf), i)) for i in range(2)]
    for i in range(2):
        for p in range(0, 8, 2):
            t = low(dot(gbt[i * hd:i * hd + hd, :], act[:, p * pf:p * pf + 2 * pf]))
            down_part(i, p)[...] = t[:, :pf]
            down_part(i, p + 1)[...] = t[:, pf:]
        jd[i].start()

    nt = nl[...].T
    for j in range(chunks):
        at = slice(j * FC, j * FC + FC)
        gu = low(dot(gb, wd[at, :], NT) * fac[:, at].astype(F32))
        bup = total(gu.astype(F32))
        for i in range(FC // 128):
            k = j * FC + 128 * i
            fv[8 + k // d:9 + k // d, k % d:k % d + 128] = bup[:, 128 * i:128 * i + 128]
        acc[...] += dot(gu, wu[:, at], NT)
        gwu[:, at] = low(dot(nt, gu))
        if j == 2:
            ju[0].start()
            jd[1].next1()
            jd[0].next1()
        if j == 3:
            back(om, out_z, so, ro, True)
    ju[1].start()

    def norm1_back(i, _):
        at = pl.ds(pl.multiple_of(i * hp, 16), hp)
        gn = acc[at]
        n1 = n1_s[at]
        fv[3:4, :] += total(gn * n1)
        fv[4:5, :] += total(gn)
        gh = norm_back(gn, n1, inv1[at, 0:1], row(g1))
        n1_s[at] = gh
        ga = low(gh)
        fv[5:6, :] += total(ga.astype(F32))
        nl[at] = ga
        return 0

    lax.fori_loop(0, nb, norm1_back, 0)
    ga = nl[...]
    datt = low(dot(ga, wo[...], NT))
    for p in range(pairs):
        dop = datt[:, 128 * p:128 * p + 128]
        prod = dop.astype(F32) * o_s[p]
        for e in range(2):
            aux = auxes[e]
            hi, mid, lo = split3(jnp.sum(jnp.where(own[e], prod, 0.0), axis=1, keepdims=True))
            tail = jnp.where(lane == aux, -hi, jnp.where(lane == aux + 1, -mid, jnp.where(lane == aux + 2, -lo, 0.0)))
            k = 128 * (2 * p + e)
            da[:, k:k + 128] = dop * own_m[e] + low(tail)
    at_ = ab[...].T
    q3 = 3 * d
    hq = q3 // 2
    gwo = low(dot(at_, ga))
    gq[:, hq:hq + hd] = gwo[:, :hd]
    gq[:, 2 * hq + hd:2 * hq + 2 * hd] = gwo[:, hd:]

    plane = [((lax.rem(lax.div(dp, 2) + n, nq) * 2 + c), z) for n in range(1, nq)]
    column = [(dp, lax.rem(z + n, nb)) for n in range(1, nb)]

    def exchange(src, got, sems, first, to, start):
        for n, t in enumerate(to):
            cp = link(src, got.at[first + n], sems, first + n, t)
            cp.start() if start else cp.wait()
        if not start:
            v = src[...]
            for n in range(len(to)):
                v = v + got[first + n]
            src[...] = v

    def vec_step(n):
        mine = pl.ds(pl.multiple_of(8 * c, 8), 8)
        other = pl.ds(pl.multiple_of(8 - 8 * c, 8), 8)
        halves = link(fv.at[other], rv.at[0], vsem, 0, peer)
        back_ = link(vhalf, fv.at[mine], vsem, nq + nb - 1, peer)
        if n == 0:
            halves.start()
        elif n == 1:
            halves.wait()
            vhalf[...] = fv[mine] + rv[0]
            exchange(vhalf, rv, vsem, 1, plane, True)
        elif n == 2:
            exchange(vhalf, rv, vsem, 1, plane, False)
            exchange(vhalf, rv, vsem, nq, column, True)
        elif n == 3:
            exchange(vhalf, rv, vsem, nq, column, False)
            back_.start()
        else:
            back_.wait()
            fv[mine] = vhalf[...]

    def vec2_step(n):
        groups = [(0, [peer]), (1, plane), (nq, column)]
        if n > 0:
            exchange(vec2, rv2, vsem2, *groups[n - 1], False)
        if n < 3:
            exchange(vec2, rv2, vsem2, *groups[n], True)

    def kvcopy(p):
        src = wd.at[pl.ds(pl.multiple_of(p * 512, 16), rows), pl.ds(0, 256)]
        return pltpu.make_async_remote_copy(src_ref=src, dst_ref=kvrecv.at[p], send_sem=kvsem.at[0, p],
                                            recv_sem=kvsem.at[1, p], device_id=peer, device_id_type=MESH)

    def pair_step(p, _):
        dq = [None, None]
        for n in range(2):
            h = (1 - c) if n == 0 else c
            kp = kall[p, h]
            vp = vall[p, h]
            bias = kb[pl.ds(pl.multiple_of(h * rows, 16), rows), :]
            kt = kp.T
            dks, dvs = [], []
            for e in range(2):
                kx = kp * own_m[e] + (bias * at_aux(e, 0, 0) + at_aux(e, 1, 3))
                vx = vp * own_m[e] + at_aux(e, 0, 2)
                q = qa[2 * p + e]
                do = da[:, pl.ds(pl.multiple_of((2 * p + e) * 128, 128), 128)]
                pt = jnp.exp(dot(kx, q, NT))
                ds = low(pt * dot(vx, do, NT))
                dvs.append(dot(low(pt), do))
                dks.append(dot(ds, q))
                t = dot(kt[64 * e:64 * e + 64, :], ds)
                dq[e] = t if dq[e] is None else dq[e] + t
            dk = jnp.where(lane < 64, dks[0], dks[1])
            dv = jnp.where(lane < 64, dvs[0], dvs[1])
            if n == 0:
                at = pl.ds(pl.multiple_of(p * 512, 16), rows)
                wd[at, 0:128] = low(dk)
                wd[at, 128:256] = low(dv)
                kvcopy(p).start()
            else:
                o_s[p] = dk
                acc[:, pl.ds(pl.multiple_of(p * 128, 128), 128)] = dv
        dqp = jnp.concatenate(dq, axis=0).T * 0.125
        dqkv[:, pl.ds(pl.multiple_of(p * 128, 128), 128)] = low(dqp)
        return 0

    part_q = [(0, 2 * hd), (2 * hd, hq + hd)]
    jq = []
    for t in range(2):
        for i in range(2):
            at0 = t * (hq + hd) + i * 2 * hd
            jq.append(make(4 + 2 * t + i, ((0, 1, 2), (0, 2, 1))[i], functools.partial(
                lambda at0, p: rows_of(gq, p, at0, 2 * hd), at0)))
    half = pairs // 2

    def finish_pairs(t):
        for p in range(t * half, t * half + half):
            kvcopy(p).wait()
            dqkv[:, d + 128 * p:d + 128 * p + 128] = low(o_s[p] + kvrecv[p, :, 0:128].astype(F32))
            dqkv[:, 2 * d + 128 * p:2 * d + 128 * p + 128] = low(
                acc[:, 128 * p:128 * p + 128] + kvrecv[p, :, 128:256].astype(F32))
        xt = xm[...].reshape(rows, d).T
        for n in range(3):
            at = t * (hq + hd) + n * hd
            gq[:, at:at + hd] = low(dot(xt, dqkv[:, n * d + t * hd:n * d + t * hd + hd]))
            if n == 1:
                jq[2 * t].start()
        jq[2 * t + 1].start()

    zd = Pieces(dp, z, nbits, *zbufs[0:4], jsem[8])
    zu = Pieces(dp, z, nbits, *zbufs[4:8], jsem[9])
    zq = [Pieces(dp, z, nbits, *zbufs[8 + 4 * i:12 + 4 * i], jsem[10 + i]) for i in range(2)]

    pr_z = d // nb

    def at_p(k, what):
        def f(p):
            @pl.when(p == k)
            def _():
                what()
        return f

    def start_down():
        vd = jnp.concatenate([jd[0].result(), jd[1].result()], axis=0)
        for j in range(nb):
            zd.zs[j % 2, j // 2] = low(vd[pr_z * j:pr_z * j + pr_z, :])
        zd.start()

    def start_up():
        vu = [ju[0].result(), ju[1].result()]
        n = ff // nb
        for j in range(nb):
            k = j * n
            zu.zs[j % 2, j // 2] = low(vu[k // hf][:, k % hf:k % hf + n])
        zu.start()

    def step1():
        vec_step(1)
        ju[1].next1()

    def step2():
        ju[0].next1()

    def step3():
        vec_step(2)

    def step4():
        weights[0].start()

    def step5():
        finish_pairs(0)
        jd[1].next2()
        vec_step(3)

    vec_step(0)
    todo = [at_p(1, step1), at_p(2, step2), at_p(3, step3), at_p(4, step4), at_p(5, step5)]

    def step(p, carry):
        for t in todo:
            t(p)
        return pair_step(p, carry)

    lax.fori_loop(0, pairs, step, 0)
    jd[0].next2()
    finish_pairs(1)
    vec_step(4)
    weights[0].wait()
    for n in range(3):
        n1_s[...] += dot(dqkv[:, n * d:n * d + d], wq[:, n * d:n * d + d], NT)
    dxs[...] = low(n1_s[...]).reshape(dxs.shape)
    back(dxs, dx_z, sd, rd, True)
    third = d // 3
    for n, k in ((0, 0), (1, 2 * d)):
        t = total(dqkv[:, k:k + d].astype(F32))
        for i in range(3):
            vec2[3 * n + i:3 * n + i + 1, :] = t[:, third * i:third * i + third]
    vec2[6:8, :] = jnp.zeros((2, third), F32)
    vec2_step(0)
    ju[1].next2()
    ju[0].next2()
    start_down()
    jq[3].next1()
    jq[2].next1()
    vec2_step(1)
    start_up()
    jq[1].next1()
    jq[0].next1()
    jq[3].next2()
    vec2_step(2)
    zd.next1()
    jq[2].next2()
    jq[0].next2()
    jq[1].next2()
    zu.next1()
    va = [jq[0].result(), jq[1].result()]
    vb = [jq[2].result(), jq[3].result()]
    cols = []
    for i, k in ((0, 0), (0, 1), (1, 0), (1, 1)):
        cols += [va[i][:, k * hd:k * hd + hd], vb[i][:, k * hd:k * hd + hd]]
    v = jnp.concatenate(cols, axis=1)
    left = pltpu.roll(v, v.shape[1] - 64, 1)
    right = pltpu.roll(v, 64, 1)
    wide = q3 // nb
    cut = wide - 64
    lane_p = lane_of((pr, 128))
    for j in range(nb):
        s0, s1_ = wide * j, q3 + d // nb * j
        a = v[:, s0:s0 + wide + 64] if j % 2 == 0 else left[:, s0 - 64:s0 + wide]
        b = right[:, s1_:s1_ + 256] if j % 2 == 0 else v[:, s1_ - 64:s1_ + 192]
        piece = low(jnp.concatenate([a[:, :cut], jnp.where(lane_p < 64, a[:, cut:], b[:, :128]), b[:, 128:]], axis=1))
        for i in range(2):
            zq[i].zs[j % 2, j // 2] = piece[pr // 2 * i:pr // 2 * i + pr // 2]
    zq[0].start()
    zq[1].start()
    vec2_step(3)
    for n in range(2):
        for i in range(3):
            fv[12 + n:13 + n, third * i:third * i + third] = vec2[3 * n + i:3 * n + i + 1, :]
    fd[...] = zd.result()
    zq[0].next1()
    fu[...] = zu.result()
    zq[1].next1()
    back(om, out_z, so, ro, False)
    back_in(om, out_z, ro)
    back(dxs, dx_z, sd, rd, False)
    back_in(dxs, dx_z, rd)
    for i in range(2):
        fq[pr // 2 * i:pr // 2 * i + pr // 2, :] = zq[i].result()


def layer(nbits, nb, lengths, speech, grad_output, vectors, w_qkv, w_out, w_up, w_down):
    blk_len, d = speech.shape[1:]
    hp = -(-blk_len // 32) * 16
    heads = d // 64
    rows = nb * hp
    pairs = d // 128
    ff = w_up.shape[1]
    pr, pf = d // 8, ff // 8
    wide = 4 * d // nb
    extra = nbits - 3
    nq = (1 << nbits) // 2
    out = [
        jax.ShapeDtypeStruct((2, 2 * hp, d), BF16),
        jax.ShapeDtypeStruct((2, 2 * hp, d), BF16),
        jax.ShapeDtypeStruct((d // nb, pf), F32),
        jax.ShapeDtypeStruct((pr, ff // nb), F32),
        jax.ShapeDtypeStruct((pr, wide), F32),
        jax.ShapeDtypeStruct((16, d), F32),
    ]
    dma = pltpu.SemaphoreType.DMA

    def job(r, c):
        return [VMEM((2, 2, r, c), BF16), VMEM((2, r, c), BF16), VMEM((r, c), BF16)]

    def pieces(r, c):
        more = (extra, r, c) if extra else (8, 128)
        return [VMEM((2, 2, r, c), BF16), VMEM((2, r, c), BF16), VMEM((r, c), BF16), VMEM(more, BF16)]

    scratch = [
        VMEM(w_qkv.shape, BF16), VMEM(w_out.shape, BF16), VMEM(w_up.shape, BF16), VMEM(w_down.shape, BF16),
        VMEM((nb, hp, d), BF16), VMEM((nb, hp, d), BF16), VMEM((nb, hp, d), BF16),
        VMEM((heads, rows, 128), BF16), VMEM((pairs, 2, rows, 128), BF16), VMEM((pairs, 2, rows, 128), BF16),
        VMEM((2 * rows, 128), BF16), VMEM((pairs, rows, 128), F32), VMEM((rows, d), BF16),
        VMEM((rows, d), BF16), VMEM((rows, 128), F32),
        VMEM((rows, ff), BF16), VMEM((rows, ff), BF16),
        VMEM((rows, d), F32), VMEM((rows, d), F32),
        VMEM((d // 2, ff), BF16), VMEM((d, ff), BF16), VMEM((pairs, rows, 256), BF16),
        VMEM((2, 2, 8, 128), F32), VMEM((nq + nb - 1, 8, d), F32), VMEM((8, d), F32),
        VMEM((nq + nb - 1, 8, d // 3), F32), VMEM((8, d // 3), F32),
    ]
    scratch += job(d // 2, pf) * 2 + job(pr, ff // 2) * 2 + job(pr, d) * 4
    scratch += pieces(d // nb, pf) + pieces(pr, ff // nb) + pieces(pr // 2, wide) * 2
    scratch += [dma((4,)), dma((2,)), dma((2, pairs)), dma((2, 2, pairs)), dma((2, nq + nb)), dma((2, nq + nb - 1))]
    scratch += [dma((4,))] * 8
    scratch += [dma((2, 6))] * 8 + [dma((2, 2 + extra))] * 4
    return pl.pallas_call(
        functools.partial(layer_kernel, (nb, hp, nbits, heads)),
        name="layer",
        out_shape=out,
        in_specs=[pl.BlockSpec(memory_space=pltpu.SMEM)] + [VM] * 11 + [ANY] * 4,
        out_specs=[VM] * len(out),
        scratch_shapes=scratch,
        compiler_params=pltpu.CompilerParams(collective_id=0, has_side_effects=True, vmem_limit_bytes=64 << 20),
    )(lengths, speech, grad_output, *vectors, w_qkv, w_out, w_up, w_down)


def finish_kernel(blk_len, cols, out_z, dx_z, fd, fu, fq, fv, out, dx, gq, bq, bv, go, bo, g1, s1, gu, bu, gd, bd, g2, s2):
    wq, wo = cols
    d = dx.shape[2]
    out[...] = out_z[:, :blk_len]
    dx[...] = dx_z[:, :blk_len].astype(F32)
    gq[...] = fq[:, :wq]
    go[...] = pltpu.roll(fq[:, wq - 64:], 192, 1)[:, :wo]
    gu[...] = fu[...]
    gd[...] = fd[...]
    for ref, n in ((g2, 0), (s2, 1), (bd, 2), (g1, 3), (s1, 4), (bo, 5), (bq, 12), (bv, 13)):
        ref[...] = fv[n:n + 1, :].reshape(d)
    for n in range(bu.shape[0] // d):
        bu[d * n:d * n + d] = fv[8 + n:9 + n, :].reshape(d)


def shards(speech, lengths, grad_output, w_qkv, bias_query, bias_value, w_out, bias_out, gain_first, shift_first,
           w_up, bias_up, w_down, bias_down, gain_second, shift_second):
    utts, blk_len, d = speech.shape
    nb = lax.axis_size("blk")
    ndp = lax.axis_size("dp")
    nbits = ndp.bit_length() - 1
    ff = bias_up.shape[0]
    vectors = (bias_query, bias_value, bias_out, gain_first, shift_first, bias_up, bias_down, gain_second, shift_second)
    got = layer(nbits, nb, lengths, speech, grad_output, vectors, w_qkv, w_out, w_up, w_down)
    wq, wo = 3 * d // nb, d // nb
    shape = jax.ShapeDtypeStruct
    vec = shape((d,), F32)
    res = pl.pallas_call(
        functools.partial(finish_kernel, blk_len, (wq, wo)),
        name="finish",
        out_shape=[
            shape((utts, blk_len, d), BF16), shape((utts, blk_len, d), F32), shape((d // 8, wq), F32), vec, vec,
            shape((d // 8, wo), F32), vec, vec, vec, shape((d // 8, ff // nb), F32), shape((ff,), F32),
            shape((wo, ff // 8), F32), vec, vec, vec,
        ],
        in_specs=[VM] * 6,
        out_specs=[VM] * 15,
        compiler_params=pltpu.CompilerParams(vmem_limit_bytes=60 << 20),
    )(*got)
    res = list(res)
    res[11] = res[11].T
    parts = ndp // 8
    if parts > 1:
        sub = lax.rem(lax.axis_index("dp"), parts)
        for i in (2, 5, 9, 11):
            n = res[i].shape[0] // parts
            res[i] = lax.dynamic_slice_in_dim(res[i], sub * n, n, 0)
    return tuple(res)


def solution(mesh):
    rows = P("dp", "blk", None)
    cut = P("dp", "blk")
    return jax.shard_map(
        shards,
        mesh=mesh,
        in_specs=(rows, P("dp"), rows) + (P(),) * 13,
        out_specs=(rows, rows, cut, P(), P(), cut, P(), P(), P(), cut, P(), cut, P(), P(), P()),
        check_vma=False,
    )
```

```python
import functools

import jax
import jax.numpy as jnp
from jax import lax
from jax.experimental import pallas as pl
from jax.experimental.pallas import tpu as pltpu
from jax.sharding import PartitionSpec as P

MESH = pl.DeviceIdType.MESH
VMEM = pltpu.VMEM
F32, BF16 = jnp.float32, jnp.bfloat16
EPS = 1e-05
MASKED = -1000000000.0
FC = 512
NN = (((1,), (0,)), ((), ()))
NT = (((1,), (1,)), ((), ()))
ANY = pl.BlockSpec(memory_space=pl.ANY)
VM = pl.BlockSpec(memory_space=pltpu.VMEM)


def dot(a, b, dims=NN):
    return lax.dot_general(a, b, dims, preferred_element_type=F32)


def low(v):
    return v.astype(BF16)


def total(v):
    return jnp.sum(v, axis=0, keepdims=True)


def split3(v):
    hi = low(v)
    rest = v - hi.astype(F32)
    mid = low(rest)
    return hi.astype(F32), mid.astype(F32), rest - mid.astype(F32)


def lane_of(shape):
    return lax.broadcasted_iota(jnp.int32, shape, len(shape) - 1)


def bit_of(v, k):
    return lax.rem(lax.div(v, 1 << k), 2)


def flip(v, k):
    return v + (1 << k) - (2 << k) * bit_of(v, k)


def norm(v, gain, shift):
    mean = jnp.mean(v, axis=1, keepdims=True)
    cen = v - mean
    inv = lax.rsqrt(jnp.mean(cen * cen, axis=1, keepdims=True) + EPS)
    n = cen * inv
    return n * gain + shift, n, inv


def norm_back(up, n, inv, gain):
    s = up * gain
    return inv * (s - jnp.mean(s, axis=1, keepdims=True) - n * jnp.mean(s * n, axis=1, keepdims=True))


def link(src, dst, sems, n, to):
    return pltpu.make_async_remote_copy(src_ref=src, dst_ref=dst, send_sem=sems.at[0, n], recv_sem=sems.at[1, n],
                                        device_id=to, device_id_type=MESH)


class Halving:
    def __init__(self, dp, z, nbits, order, part, r0, r1, r2, sems):
        self.dp, self.z, self.order, self.part = dp, z, order, part
        self.r0, self.r1, self.r2, self.sems = r0, r1, r2, sems
        self.bits = [nbits - 3 + k for k in order]
        self.mine = [bit_of(dp, t) for t in self.bits]

    def at(self, m, a, b):
        k0, k1, k2 = self.order
        return self.part(m * (1 << k0) + a * (1 << k1) + b * (1 << k2))

    def copies(self, stage):
        to = (flip(self.dp, self.bits[stage]), self.z)
        m = self.mine
        if stage == 0:
            return [link(self.at(1 - m[0], a, b), self.r0.at[a, b], self.sems, 2 * a + b, to)
                    for a in range(2) for b in range(2)]
        if stage == 1:
            return [link(self.r0.at[1 - m[1]], self.r1, self.sems, 4, to)]
        return [link(self.r0.at[m[1], 1 - m[2]], self.r2, self.sems, 5, to)]

    def start(self):
        for c in self.copies(0):
            c.start()

    def next1(self):
        for c in self.copies(0):
            c.wait()
        m = self.mine
        for a in (1 - m[1], m[1]):
            for b in range(2):
                self.r0[a, b] = self.r0[a, b] + self.at(m[0], a, b)[...]
            if a is not m[1]:
                for c in self.copies(1):
                    c.start()

    def next2(self):
        for c in self.copies(1):
            c.wait()
        m1, m2 = self.mine[1:]
        self.r0[m1, 1 - m2] = self.r0[m1, 1 - m2] + self.r1[1 - m2]
        for c in self.copies(2):
            c.start()
        self.r0[m1, m2] = self.r0[m1, m2] + self.r1[m2]

    def result(self):
        for c in self.copies(2):
            c.wait()
        return self.r0[self.mine[1], self.mine[2]].astype(F32) + self.r2[...].astype(F32)


class Pieces:
    def __init__(self, dp, z, nbits, zs, r1, r2, rx, sems):
        self.zs, self.r1, self.r2, self.rx, self.sems = zs, r1, r2, rx, sems
        self.more = [(flip(dp, t), z) for t in range(nbits - 3)]
        self.b = [bit_of(z, 0), bit_of(z, 1)]
        self.to = [(dp, flip(z, 0)), (dp, flip(z, 1))]

    def first(self):
        return link(self.zs.at[1 - self.b[0]], self.r1, self.sems, 0, self.to[0])

    def second(self):
        return link(self.zs.at[self.b[0], 1 - self.b[1]], self.r2, self.sems, 1, self.to[1])

    def start(self):
        self.first().start()

    def next1(self):
        self.first().wait()
        b0, b1 = self.b
        self.zs[b0, 1 - b1] = self.zs[b0, 1 - b1] + self.r1[1 - b1]
        self.second().start()

    def result(self):
        self.second().wait()
        b0, b1 = self.b
        v = self.zs[b0, b1].astype(F32) + self.r1[b1].astype(F32) + self.r2[...].astype(F32)
        for n, to in enumerate(self.more):
            self.zs[b0, b1] = low(v)
            c = link(self.zs.at[b0, b1], self.rx.at[n], self.sems, 2 + n, to)
            c.start()
            c.wait()
            v = v + self.rx[n].astype(F32)
        return v


def layer_kernel(geo, len_ref, x_ref, g_ref, bq, bv, bo, g1, s1, bu, bd, g2, s2, wq_hbm, wo_hbm, wu_hbm, wd_hbm,
                 out_hbm, dx_hbm, fd, fu, fq, fv, out_z, dx_z, osem, *scratch):
    nb, hp, nbits, heads = geo
    (wq, wo, wu, wd, xm, gm, om, qa, kall, vall, kb, o_s, ab, nl, inv1, act, fac, n1_s, acc, gwd, gwu, kvrecv, lens, rv, vhalf, rv2, vec2,
     *rest) = scratch
    jobs, rest = rest[:24], rest[24:]
    zbufs, (wsem, lsem, kvsem, kvs2, vsem, vsem2, sx, rx, sg, rg, so, ro, sd, rd, *jsem) = rest[:16], rest[16:]
    blk_len, d = x_ref.shape[1:]
    dp, z = lax.axis_index("dp"), lax.axis_index("blk")
    c = lax.rem(dp, 2)
    base = dp - c
    peer = (base + 1 - c, z)
    rows, ff = act.shape
    nq = (1 << nbits) // 2
    pairs = d // 128
    chunks = ff // FC
    gq = wu
    da = fac
    dqkv = act
    dxs = gm

    weights = [pltpu.make_async_copy(a, b, wsem.at[n])
               for n, (a, b) in enumerate(((wq_hbm, wq), (wo_hbm, wo), (wu_hbm, wu), (wd_hbm, wd)))]
    weights[0].start()

    barrier = pltpu.get_barrier_semaphore()
    greet = [(base + lax.rem(c + dc, 2), lax.rem(z + dz, nb)) for dz in range(nb) for dc in range(2) if dz or dc]
    greet += [(lax.rem(lax.div(dp, 2) + n, nq) * 2 + c, z) for n in range(1, nq)]
    for to in greet:
        pl.semaphore_signal(barrier, inc=1, device_id=to, device_id_type=MESH)

    def fill(src, dst):
        for s in range(2):
            dst[s, 2 * hp - 16:, :] = jnp.zeros((16, d), BF16)
            dst[s, 0:blk_len, :] = src[s]

    fill(x_ref, out_z)
    for s in range(2):
        lens[c, s] = jnp.full((8, 128), len_ref[s], jnp.int32).astype(F32)
    pl.semaphore_wait(barrier, len(greet))

    lcopy = pltpu.make_async_remote_copy(src_ref=lens.at[c], dst_ref=lens.at[c], send_sem=lsem.at[0],
                                         recv_sem=lsem.at[1], device_id=peer, device_id_type=MESH)

    def spread(src, dst, ss, rs, start):
        for s in range(2):
            for h in range(2):
                to = 2 * c + s
                here = jnp.logical_and(to == z, c == h)
                part = src.at[s, pl.ds(h * hp, hp)]
                remote = pltpu.make_async_remote_copy(
                    src_ref=part, dst_ref=dst.at[z], send_sem=ss.at[2 * s + h], recv_sem=rs.at[z],
                    device_id=(base + h, to), device_id_type=MESH)

                @pl.when(jnp.logical_not(here))
                def _():
                    remote.start() if start else remote.wait_send()

                if start:
                    @pl.when(here)
                    def _():
                        pltpu.make_async_copy(part, dst.at[z], rs.at[z]).start()

    def spread_in(src, dst, rs):
        for i in range(nb):
            pltpu.make_async_copy(src.at[0, pl.ds(0, hp)], dst.at[i], rs.at[i]).wait()

    def back(src, dst, ss, rs, start):
        for b in range(nb):
            to_c = lax.div(z, 2)
            here = jnp.logical_and(z == b, c == to_c)
            land = dst.at[lax.rem(z, 2), pl.ds(pl.multiple_of(c * hp, 16), hp)]
            n = 2 * lax.rem(z, 2) + c
            remote = pltpu.make_async_remote_copy(src_ref=src.at[b], dst_ref=land, send_sem=ss.at[b],
                                                  recv_sem=rs.at[n], device_id=(base + to_c, jnp.int32(b)),
                                                  device_id_type=MESH)

            @pl.when(jnp.logical_not(here))
            def _():
                remote.start() if start else remote.wait_send()

            if start:
                @pl.when(here)
                def _():
                    pltpu.make_async_copy(src.at[b], land, rs.at[n]).start()

    def back_in(src, dst, rs):
        for n in range(4):
            pltpu.make_async_copy(src.at[0], dst.at[n // 2, pl.ds((n % 2) * hp, hp)], rs.at[n]).wait()

    lane1 = lane_of((1, 128))
    lane = lane_of((rows, 128))
    own = [lane1 < 64, lane1 >= 64]
    own_m = [low(o.astype(F32)) for o in own]
    auxes = (64, 0)

    def at_aux(e, lo, hi):
        return low(jnp.logical_and(lane1 >= auxes[e] + lo, lane1 <= auxes[e] + hi).astype(F32))

    row = lambda ref: ref[...].reshape(1, ref.shape[0])

    spread(out_z, xm, sx, rx, True)
    lcopy.start()
    fill(g_ref, dx_z)
    weights[0].wait()
    for w in weights[1:]:
        w.start()
    spread_in(out_z, xm, rx)
    spread(out_z, xm, sx, rx, False)
    spread(dx_z, gm, sg, rg, True)
    x = xm[...].reshape(rows, d)

    def kv_in(n, p):
        scr = (kall, vall)[n]
        return pltpu.make_async_remote_copy(src_ref=scr.at[p, c], dst_ref=scr.at[p, c], send_sem=kvs2.at[0, n, p],
                                            recv_sem=kvs2.at[1, n, p], device_id=peer, device_id_type=MESH)

    for p in range(pairs // 2):
        for n, scr in enumerate((kall, vall)):
            at = (n + 1) * d + 256 * p
            t = dot(x, wq[:, at:at + 256])
            if n == 1:
                t = t + row(bv)[:, 256 * p:256 * p + 256]
            t = low(t)
            for e in range(2):
                scr[2 * p + e, c] = t[:, 128 * e:128 * e + 128]
                kv_in(n, 2 * p + e).start()
    for p in range(pairs // 2):
        at = 256 * p
        t = low(dot(x, wq[:, at:at + 256]) + row(bq)[:, at:at + 256])
        t = low(t.astype(F32) * 0.125)
        for q in range(2):
            for e in range(2):
                qa[2 * (2 * p + q) + e] = t[:, 128 * q:128 * q + 128] * own_m[e] + at_aux(e, 0, 0)
    lcopy.wait()
    usable_len = lens[lax.div(z, 2), lax.rem(z, 2)][0:1]
    for h in range(2):
        for b in range(nb):
            t = lax.broadcasted_iota(jnp.int32, (hp, 128), 0) + h * hp
            frame = (t + blk_len * b).astype(F32)
            ok = jnp.logical_and(t < blk_len, frame < usable_len)
            kb[pl.ds((h * nb + b) * hp, hp), :] = low(jnp.where(ok, 0.0, MASKED))

    def attend_step(p, _):
        for n in range(2):
            kv_in(n, p).wait()
        kp = kall[p].reshape(2 * rows, 128)
        vp = vall[p].reshape(2 * rows, 128)
        bias = kb[...]
        outs = []
        for e in range(2):
            aux = auxes[e]
            first = at_aux(e, 0, 0)
            ka = kp * own_m[e] + bias * first
            va = vp * own_m[e] + first
            qx = qa[2 * p + e]
            s = dot(qx, ka, NT)
            m = jnp.max(s, axis=1, keepdims=True)
            oa = dot(low(jnp.exp(s - m)), va)
            tot = oa[:, aux:aux + 1]
            outs.append(oa * (1.0 / tot))
            hi, mid, lo = split3(m + jnp.log(tot))
            tail = jnp.where(lane == aux + 1, -hi, jnp.where(lane == aux + 2, -mid, jnp.where(lane == aux + 3, -lo, 0.0)))
            qa[2 * p + e] = qx + low(tail)
        o_s[p] = jnp.where(lane < 64, outs[0], outs[1])
        return 0

    lax.fori_loop(0, pairs, attend_step, 0, unroll=2)

    for p in range(pairs):
        ab[:, 128 * p:128 * p + 128] = low(o_s[p])
    weights[1].wait()
    acc[...] = dot(ab[...], wo[...])

    def norm1(i, _):
        at = pl.ds(pl.multiple_of(i * hp, 16), hp)
        normed, n, inv = norm(xm[i].astype(F32) + acc[at] + row(bo), row(g1), row(s1))
        n1_s[at] = n
        inv1[at] = jnp.broadcast_to(inv, (hp, 128))
        acc[at] = normed + row(bd)
        nl[at] = low(normed)
        return 0

    lax.fori_loop(0, nb, norm1, 0)
    weights[2].wait()
    weights[3].wait()

    for j in range(chunks):
        at = slice(j * FC, j * FC + FC)
        u = dot(nl[...], wu[:, at]) + row(bu)[:, at]
        cdf = 0.5 + 0.5 * lax.erf(u * 0.7071067811865476)
        dens = jnp.exp(-0.5 * u * u) * 0.3989422804014327
        a = low(u * cdf)
        act[:, at] = a
        fac[:, at] = low(cdf + u * dens)
        acc[...] += dot(a, wd[at, :])
    spread_in(dx_z, gm, rg)
    spread(dx_z, gm, sg, rg, False)
    fv[...] = jnp.zeros(fv.shape, F32)

    def norm2(i, _):
        at = pl.ds(pl.multiple_of(i * hp, 16), hp)
        result, n2, inv2 = norm(acc[at], row(g2), row(s2))
        om[i] = low(result)
        g = gm[i].astype(F32)
        fv[0:1, :] += total(g * n2)
        fv[1:2, :] += total(g)
        back2 = norm_back(g, n2, inv2, row(g2))
        acc[at] = back2
        gb = low(back2)
        fv[2:3, :] += total(gb.astype(F32))
        gm[i] = gb
        return 0

    lax.fori_loop(0, nb, norm2, 0)
    gb = gm[...].reshape(rows, d)
    gbt = gb.T

    def make(n, order, part):
        return Halving(dp, z, nbits, order, part, *jobs[3 * n:3 * n + 3], jsem[n])

    pr, pf = d // 8, ff // 8
    hd, hf = d // 2, ff // 2
    rows_of = lambda ref, p, at, n: ref.at[pl.ds(pl.multiple_of(p * pr, 16), pr), pl.ds(at, n)]
    def down_part(i, p):
        if i == 0:
            return gwd.at[:, pl.ds(pl.multiple_of(p * pf, 128), pf)]
        across = wq.shape[1] // pf
        return wq.at[pl.ds(pl.multiple_of(lax.div(p, across) * hd, 16), hd),
                     pl.ds(pl.multiple_of(lax.rem(p, across) * pf, 128), pf)]

    jd = [make(i, ((0, 1, 2), (0, 2, 1))[i], functools.partial(down_part, i)) for i in range(2)]
    ju = [make(2 + i, ((0, 2, 1), (0, 1, 2))[i], functools.partial(
        lambda i, p: rows_of(gwu, p, i * hf, hf), i)) for i in range(2)]
    for i in range(2):
        for p in range(0, 8, 2):
            t = low(dot(gbt[i * hd:i * hd + hd, :], act[:, p * pf:p * pf + 2 * pf]))
            down_part(i, p)[...] = t[:, :pf]
            down_part(i, p + 1)[...] = t[:, pf:]
        jd[i].start()

    nt = nl[...].T
    for j in range(chunks):
        at = slice(j * FC, j * FC + FC)
        gu = low(dot(gb, wd[at, :], NT) * fac[:, at].astype(F32))
        bup = total(gu.astype(F32))
        for i in range(FC // 128):
            k = j * FC + 128 * i
            fv[8 + k // d:9 + k // d, k % d:k % d + 128] = bup[:, 128 * i:128 * i + 128]
        acc[...] += dot(gu, wu[:, at], NT)
        gwu[:, at] = low(dot(nt, gu))
        if j == 2:
            ju[0].start()
            jd[1].next1()
            jd[0].next1()
        if j == 3:
            back(om, out_z, so, ro, True)
    ju[1].start()

    def norm1_back(i, _):
        at = pl.ds(pl.multiple_of(i * hp, 16), hp)
        gn = acc[at]
        n1 = n1_s[at]
        fv[3:4, :] += total(gn * n1)
        fv[4:5, :] += total(gn)
        gh = norm_back(gn, n1, inv1[at, 0:1], row(g1))
        n1_s[at] = gh
        ga = low(gh)
        fv[5:6, :] += total(ga.astype(F32))
        nl[at] = ga
        return 0

    lax.fori_loop(0, nb, norm1_back, 0)
    ga = nl[...]
    datt = low(dot(ga, wo[...], NT))
    for p in range(pairs):
        dop = datt[:, 128 * p:128 * p + 128]
        prod = dop.astype(F32) * o_s[p]
        for e in range(2):
            aux = auxes[e]
            hi, mid, lo = split3(jnp.sum(jnp.where(own[e], prod, 0.0), axis=1, keepdims=True))
            tail = jnp.where(lane == aux, -hi, jnp.where(lane == aux + 1, -mid, jnp.where(lane == aux + 2, -lo, 0.0)))
            k = 128 * (2 * p + e)
            da[:, k:k + 128] = dop * own_m[e] + low(tail)
    at_ = ab[...].T
    q3 = 3 * d
    hq = q3 // 2
    gwo = low(dot(at_, ga))
    gq[:, hq:hq + hd] = gwo[:, :hd]
    gq[:, 2 * hq + hd:2 * hq + 2 * hd] = gwo[:, hd:]

    plane = [((lax.rem(lax.div(dp, 2) + n, nq) * 2 + c), z) for n in range(1, nq)]
    column = [(dp, lax.rem(z + n, nb)) for n in range(1, nb)]

    def exchange(src, got, sems, first, to, start):
        for n, t in enumerate(to):
            cp = link(src, got.at[first + n], sems, first + n, t)
            cp.start() if start else cp.wait()
        if not start:
            v = src[...]
            for n in range(len(to)):
                v = v + got[first + n]
            src[...] = v

    def vec_step(n):
        mine = pl.ds(pl.multiple_of(8 * c, 8), 8)
        other = pl.ds(pl.multiple_of(8 - 8 * c, 8), 8)
        halves = link(fv.at[other], rv.at[0], vsem, 0, peer)
        back_ = link(vhalf, fv.at[mine], vsem, nq + nb - 1, peer)
        if n == 0:
            halves.start()
        elif n == 1:
            halves.wait()
            vhalf[...] = fv[mine] + rv[0]
            exchange(vhalf, rv, vsem, 1, plane, True)
        elif n == 2:
            exchange(vhalf, rv, vsem, 1, plane, False)
            exchange(vhalf, rv, vsem, nq, column, True)
        elif n == 3:
            exchange(vhalf, rv, vsem, nq, column, False)
            back_.start()
        else:
            back_.wait()
            fv[mine] = vhalf[...]

    def vec2_step(n):
        groups = [(0, [peer]), (1, plane), (nq, column)]
        if n > 0:
            exchange(vec2, rv2, vsem2, *groups[n - 1], False)
        if n < 3:
            exchange(vec2, rv2, vsem2, *groups[n], True)

    def kvcopy(p):
        src = wd.at[pl.ds(pl.multiple_of(p * 512, 16), rows), pl.ds(0, 256)]
        return pltpu.make_async_remote_copy(src_ref=src, dst_ref=kvrecv.at[p], send_sem=kvsem.at[0, p],
                                            recv_sem=kvsem.at[1, p], device_id=peer, device_id_type=MESH)

    def pair_step(p, _):
        dq = [None, None]
        for n in range(2):
            h = (1 - c) if n == 0 else c
            kp = kall[p, h]
            vp = vall[p, h]
            bias = kb[pl.ds(pl.multiple_of(h * rows, 16), rows), :]
            kt = kp.T
            dks, dvs = [], []
            for e in range(2):
                kx = kp * own_m[e] + (bias * at_aux(e, 0, 0) + at_aux(e, 1, 3))
                vx = vp * own_m[e] + at_aux(e, 0, 2)
                q = qa[2 * p + e]
                do = da[:, pl.ds(pl.multiple_of((2 * p + e) * 128, 128), 128)]
                pt = jnp.exp(dot(kx, q, NT))
                ds = low(pt * dot(vx, do, NT))
                dvs.append(dot(low(pt), do))
                dks.append(dot(ds, q))
                t = dot(kt[64 * e:64 * e + 64, :], ds)
                dq[e] = t if dq[e] is None else dq[e] + t
            dk = jnp.where(lane < 64, dks[0], dks[1])
            dv = jnp.where(lane < 64, dvs[0], dvs[1])
            if n == 0:
                at = pl.ds(pl.multiple_of(p * 512, 16), rows)
                wd[at, 0:128] = low(dk)
                wd[at, 128:256] = low(dv)
                kvcopy(p).start()
            else:
                o_s[p] = dk
                acc[:, pl.ds(pl.multiple_of(p * 128, 128), 128)] = dv
        dqp = jnp.concatenate(dq, axis=0).T * 0.125
        dqkv[:, pl.ds(pl.multiple_of(p * 128, 128), 128)] = low(dqp)
        return 0

    part_q = [(0, 2 * hd), (2 * hd, hq + hd)]
    jq = []
    for t in range(2):
        for i in range(2):
            at0 = t * (hq + hd) + i * 2 * hd
            jq.append(make(4 + 2 * t + i, ((0, 1, 2), (0, 2, 1))[i], functools.partial(
                lambda at0, p: rows_of(gq, p, at0, 2 * hd), at0)))
    half = pairs // 2

    def finish_pairs(t):
        for p in range(t * half, t * half + half):
            kvcopy(p).wait()
            dqkv[:, d + 128 * p:d + 128 * p + 128] = low(o_s[p] + kvrecv[p, :, 0:128].astype(F32))
            dqkv[:, 2 * d + 128 * p:2 * d + 128 * p + 128] = low(
                acc[:, 128 * p:128 * p + 128] + kvrecv[p, :, 128:256].astype(F32))
        xt = xm[...].reshape(rows, d).T
        for n in range(3):
            at = t * (hq + hd) + n * hd
            gq[:, at:at + hd] = low(dot(xt, dqkv[:, n * d + t * hd:n * d + t * hd + hd]))
            if n == 1:
                jq[2 * t].start()
        jq[2 * t + 1].start()

    zd = Pieces(dp, z, nbits, *zbufs[0:4], jsem[8])
    zu = Pieces(dp, z, nbits, *zbufs[4:8], jsem[9])
    zq = [Pieces(dp, z, nbits, *zbufs[8 + 4 * i:12 + 4 * i], jsem[10 + i]) for i in range(2)]

    pr_z = d // nb

    def at_p(k, what):
        def f(p):
            @pl.when(p == k)
            def _():
                what()
        return f

    def start_down():
        vd = jnp.concatenate([jd[0].result(), jd[1].result()], axis=0)
        for j in range(nb):
            zd.zs[j % 2, j // 2] = low(vd[pr_z * j:pr_z * j + pr_z, :])
        zd.start()

    def start_up():
        vu = [ju[0].result(), ju[1].result()]
        n = ff // nb
        for j in range(nb):
            k = j * n
            zu.zs[j % 2, j // 2] = low(vu[k // hf][:, k % hf:k % hf + n])
        zu.start()

    def step1():
        vec_step(1)
        ju[1].next1()
        ju[0].next1()

    def step2():
        pass

    def step3():
        vec_step(2)

    def step4():
        weights[0].start()

    def step5():
        finish_pairs(0)
        jd[1].next2()
        vec_step(3)

    vec_step(0)
    todo = [at_p(1, step1), at_p(2, step2), at_p(3, step3), at_p(4, step4), at_p(5, step5)]

    def step(p, carry):
        for t in todo:
            t(p)
        return pair_step(p, carry)

    lax.fori_loop(0, pairs, step, 0)
    jd[0].next2()
    finish_pairs(1)
    vec_step(4)
    weights[0].wait()
    for n in range(3):
        n1_s[...] += dot(dqkv[:, n * d:n * d + d], wq[:, n * d:n * d + d], NT)
    dxs[...] = low(n1_s[...]).reshape(dxs.shape)
    back(dxs, dx_z, sd, rd, True)
    third = d // 3
    for n, k in ((0, 0), (1, 2 * d)):
        t = total(dqkv[:, k:k + d].astype(F32))
        for i in range(3):
            vec2[3 * n + i:3 * n + i + 1, :] = t[:, third * i:third * i + third]
    vec2[6:8, :] = jnp.zeros((2, third), F32)
    vec2_step(0)
    ju[1].next2()
    ju[0].next2()
    start_down()
    jq[3].next1()
    jq[2].next1()
    vec2_step(1)
    start_up()
    jq[1].next1()
    jq[0].next1()
    jq[3].next2()
    vec2_step(2)
    zd.next1()
    jq[2].next2()
    jq[0].next2()
    jq[1].next2()
    zu.next1()
    va = [jq[0].result(), jq[1].result()]
    vb = [jq[2].result(), jq[3].result()]
    cols = []
    for i, k in ((0, 0), (0, 1), (1, 0), (1, 1)):
        cols += [va[i][:, k * hd:k * hd + hd], vb[i][:, k * hd:k * hd + hd]]
    v = jnp.concatenate(cols, axis=1)
    left = pltpu.roll(v, v.shape[1] - 64, 1)
    right = pltpu.roll(v, 64, 1)
    wide = q3 // nb
    cut = wide - 64
    lane_p = lane_of((pr, 128))
    for j in range(nb):
        s0, s1_ = wide * j, q3 + d // nb * j
        a = v[:, s0:s0 + wide + 64] if j % 2 == 0 else left[:, s0 - 64:s0 + wide]
        b = right[:, s1_:s1_ + 256] if j % 2 == 0 else v[:, s1_ - 64:s1_ + 192]
        piece = low(jnp.concatenate([a[:, :cut], jnp.where(lane_p < 64, a[:, cut:], b[:, :128]), b[:, 128:]], axis=1))
        for i in range(2):
            zq[i].zs[j % 2, j // 2] = piece[pr // 2 * i:pr // 2 * i + pr // 2]
    zq[0].start()
    zq[1].start()
    vec2_step(3)
    for n in range(2):
        for i in range(3):
            fv[12 + n:13 + n, third * i:third * i + third] = vec2[3 * n + i:3 * n + i + 1, :]
    fd[...] = zd.result()
    zq[0].next1()
    fu[...] = zu.result()
    zq[1].next1()
    back(om, out_z, so, ro, False)
    back_in(om, out_z, ro)
    outs = [pltpu.make_async_copy(a, b, osem.at[n]) for n, (a, b) in enumerate(((out_z, out_hbm), (dx_z, dx_hbm)))]
    outs[0].start()
    back(dxs, dx_z, sd, rd, False)
    back_in(dxs, dx_z, rd)
    outs[1].start()
    for i in range(2):
        fq[pr // 2 * i:pr // 2 * i + pr // 2, :] = zq[i].result()
    for o in outs:
        o.wait()


def layer(nbits, nb, lengths, speech, grad_output, vectors, w_qkv, w_out, w_up, w_down):
    blk_len, d = speech.shape[1:]
    hp = -(-blk_len // 32) * 16
    heads = d // 64
    rows = nb * hp
    pairs = d // 128
    ff = w_up.shape[1]
    pr, pf = d // 8, ff // 8
    wide = 4 * d // nb
    extra = nbits - 3
    nq = (1 << nbits) // 2
    out = [
        jax.ShapeDtypeStruct((2, 2 * hp, d), BF16),
        jax.ShapeDtypeStruct((2, 2 * hp, d), BF16),
        jax.ShapeDtypeStruct((d // nb, pf), F32),
        jax.ShapeDtypeStruct((pr, ff // nb), F32),
        jax.ShapeDtypeStruct((pr, wide), F32),
        jax.ShapeDtypeStruct((16, d), F32),
    ]
    dma = pltpu.SemaphoreType.DMA

    def job(r, c):
        return [VMEM((2, 2, r, c), BF16), VMEM((2, r, c), BF16), VMEM((r, c), BF16)]

    def pieces(r, c):
        more = (extra, r, c) if extra else (8, 128)
        return [VMEM((2, 2, r, c), BF16), VMEM((2, r, c), BF16), VMEM((r, c), BF16), VMEM(more, BF16)]

    scratch = [
        VMEM((2, 2 * hp, d), BF16), VMEM((2, 2 * hp, d), BF16), dma((2,)),
        VMEM(w_qkv.shape, BF16), VMEM(w_out.shape, BF16), VMEM(w_up.shape, BF16), VMEM(w_down.shape, BF16),
        VMEM((nb, hp, d), BF16), VMEM((nb, hp, d), BF16), VMEM((nb, hp, d), BF16),
        VMEM((heads, rows, 128), BF16), VMEM((pairs, 2, rows, 128), BF16), VMEM((pairs, 2, rows, 128), BF16),
        VMEM((2 * rows, 128), BF16), VMEM((pairs, rows, 128), F32), VMEM((rows, d), BF16),
        VMEM((rows, d), BF16), VMEM((rows, 128), F32),
        VMEM((rows, ff), BF16), VMEM((rows, ff), BF16),
        VMEM((rows, d), F32), VMEM((rows, d), F32),
        VMEM((d // 2, ff), BF16), VMEM((d, ff), BF16), VMEM((pairs, rows, 256), BF16),
        VMEM((2, 2, 8, 128), F32), VMEM((nq + nb - 1, 8, d), F32), VMEM((8, d), F32),
        VMEM((nq + nb - 1, 8, d // 3), F32), VMEM((8, d // 3), F32),
    ]
    scratch += job(d // 2, pf) * 2 + job(pr, ff // 2) * 2 + job(pr, d) * 4
    scratch += pieces(d // nb, pf) + pieces(pr, ff // nb) + pieces(pr // 2, wide) * 2
    scratch += [dma((4,)), dma((2,)), dma((2, pairs)), dma((2, 2, pairs)), dma((2, nq + nb)), dma((2, nq + nb - 1))]
    scratch += [dma((4,))] * 8
    scratch += [dma((2, 6))] * 8 + [dma((2, 2 + extra))] * 4
    return pl.pallas_call(
        functools.partial(layer_kernel, (nb, hp, nbits, heads)),
        name="layer",
        out_shape=out,
        in_specs=[pl.BlockSpec(memory_space=pltpu.SMEM)] + [VM] * 11 + [ANY] * 4,
        out_specs=[ANY] * 2 + [VM] * (len(out) - 2),
        scratch_shapes=scratch,
        compiler_params=pltpu.CompilerParams(collective_id=0, has_side_effects=True, vmem_limit_bytes=64 << 20),
    )(lengths, speech, grad_output, *vectors, w_qkv, w_out, w_up, w_down)


def finish_kernel(blk_len, cols, out_z, dx_z, fd, fu, fq, fv, out, dx, gq, bq, bv, go, bo, g1, s1, gu, bu, gd, bd, g2, s2):
    wq, wo = cols
    d = dx.shape[2]
    out[...] = out_z[:, :blk_len]
    dx[...] = dx_z[:, :blk_len].astype(F32)

    @pl.when(pl.program_id(0) == 0)
    def _():
        small(fd, fu, fq, fv, wq, wo, d, gq, bq, bv, go, bo, g1, s1, gu, bu, gd, bd, g2, s2)


def small(fd, fu, fq, fv, wq, wo, d, gq, bq, bv, go, bo, g1, s1, gu, bu, gd, bd, g2, s2):
    gq[...] = fq[:, :wq]
    go[...] = pltpu.roll(fq[:, wq - 64:], 192, 1)[:, :wo]
    gu[...] = fu[...]
    gd[...] = fd[...]
    for ref, n in ((g2, 0), (s2, 1), (bd, 2), (g1, 3), (s1, 4), (bo, 5), (bq, 12), (bv, 13)):
        ref[...] = fv[n:n + 1, :].reshape(d)
    for n in range(bu.shape[0] // d):
        bu[d * n:d * n + d] = fv[8 + n:9 + n, :].reshape(d)


def shards(speech, lengths, grad_output, w_qkv, bias_query, bias_value, w_out, bias_out, gain_first, shift_first,
           w_up, bias_up, w_down, bias_down, gain_second, shift_second):
    utts, blk_len, d = speech.shape
    nb = lax.axis_size("blk")
    ndp = lax.axis_size("dp")
    nbits = ndp.bit_length() - 1
    ff = bias_up.shape[0]
    vectors = (bias_query, bias_value, bias_out, gain_first, shift_first, bias_up, bias_down, gain_second, shift_second)
    got = layer(nbits, nb, lengths, speech, grad_output, vectors, w_qkv, w_out, w_up, w_down)
    wq, wo = 3 * d // nb, d // nb
    shape = jax.ShapeDtypeStruct
    vec = shape((d,), F32)
    shapes = [
        shape((utts, blk_len, d), BF16), shape((utts, blk_len, d), F32), shape((d // 8, wq), F32), vec, vec,
        shape((d // 8, wo), F32), vec, vec, vec, shape((d // 8, ff // nb), F32), shape((ff,), F32),
        shape((wo, ff // 8), F32), vec, vec, vec,
    ]

    def one(s):
        return pl.BlockSpec((1,) + s[1:], lambda i: (i, 0, 0))

    def all_of(s):
        return pl.BlockSpec(s, lambda i: (0,) * len(s))

    res = pl.pallas_call(
        functools.partial(finish_kernel, blk_len, (wq, wo)),
        name="finish",
        out_shape=shapes,
        grid=(utts,),
        in_specs=[one(got[0].shape), one(got[1].shape)] + [all_of(a.shape) for a in got[2:]],
        out_specs=[one(a.shape) if len(a.shape) == 3 else all_of(a.shape) for a in shapes],
        compiler_params=pltpu.CompilerParams(vmem_limit_bytes=60 << 20),
    )(*got)
    res = list(res)
    res[11] = res[11].T
    parts = ndp // 8
    if parts > 1:
        sub = lax.rem(lax.axis_index("dp"), parts)
        for i in (2, 5, 9, 11):
            n = res[i].shape[0] // parts
            res[i] = lax.dynamic_slice_in_dim(res[i], sub * n, n, 0)
    return tuple(res)


def solution(mesh):
    rows = P("dp", "blk", None)
    cut = P("dp", "blk")
    return jax.shard_map(
        shards,
        mesh=mesh,
        in_specs=(rows, P("dp"), rows) + (P(),) * 13,
        out_specs=(rows, rows, cut, P(), P(), cut, P(), P(), P(), cut, P(), cut, P(), P(), P()),
        check_vma=False,
    )
```
